128 devices in a mesh: grp: 4 (over y), dom: 32 (over x, z, core).
Axes of the slice: x: 4, y: 4, z: 4, core: 2. Of those that a mesh axis runs over, the one named last changes fastest.
Arguments:
- grad_rhs: float32 [4096, 320], P(('grp', 'dom')), may hold values from -41 to 41
- block_inv: bfloat16 [4096, 320, 320], P(('grp', 'dom')), may hold values from -1 to 3
- face_jac: bfloat16 [4096, 6, 80, 80], P(('grp', 'dom')), may hold values from -0.3125 to 0.3125
- face_nbr: int32 [4096, 6], P(('grp', 'dom')), may hold values from -1 to 95, as said below
- recv_node: int32 [65536], P(('grp', 'dom')), may hold values from 0 to 2047
- owners: int32 [65536, 1], P(('grp', 'dom')), may hold values from 0 to 127; in each aligned block of 512 rows (0 to 511, 512 to 1023, ...) at most 8 rows name the same one
- donor_elem: int32 [65536], P(('grp', 'dom')), may hold values from 0 to 31
- donor_coords: float32 [3, 65536], P(None, ('grp', 'dom')), may hold values from -1 to 1
- recv_counts: int32 [128, 4], P(('grp', 'dom')), may hold values from 1 to 128, 416 in all within a row
Outputs:
- adjoint_sol: float32 [4096, 320], P(('grp', 'dom'))
The draws below stay inside these ranges and needn't reach their ends.
Inputs may be any that keep to these rules, and one draw needn't show every extreme that they name: `face_nbr`: each entry is -1 (outer boundary), an element of the same device (below 32), a low interface slot (32 to 63, facing the device one lower along dom) or a high interface slot; on each device every interface slot is named by exactly one face, local neighbours are mutual through face f xor 1, and low slot k faces high slot k of the lower device. `owners`: no owner is named by more than 8 of one device's 512 rows.
All inputs are finite; a program needn't handle non-finite values.
Results may differ from the reference program's by a relative error of at most 0.0018.
Values sent between devices are 32-bit elements; how exact they have to be, the bound alone decides.
No kernel may reach another device: no remote copies, remote signals or barrier semaphores. Data moves between devices by JAX's collectives and lax.ppermute only.
A program may use at most 64 MiB of HBM per device.

```python
import math
import jax
import jax.numpy as jnp
import numpy as np
from jax import lax

VARS = 5
NODES = 64
FNODES = 16
BLOCK = 320
FACEW = 80
ESIDE = 4
ELX = 1
NB = 4
ITERS = 2
E = 32
IFACE = 32
PEERS = 128
NE = 4096
RPTS = 512
NR = 65536
CAP = 8
N_GRP = 4
N_DOM = 32


def draw_grad_rhs(key, part):
    key = jax.random.fold_in(key, 1)
    key_base, key_rows, key_cols = jax.random.split(key, 3)
    row_scale = jnp.exp(jax.random.uniform(key_rows, (NE, 1), jnp.float32, math.log(0.1), 0.0))
    col_scale = jnp.exp(jax.random.uniform(key_cols, (1, BLOCK), jnp.float32, math.log(0.3), math.log(3.0)))
    rising = 0.5 + jnp.arange(NE, dtype=jnp.float32)[:, None] / NE
    base = jax.random.normal(key_base, (NE, BLOCK), jnp.float32)
    base = jnp.clip(base, -4.0, 4.0)
    return base * row_scale * col_scale * rising


def draw_block_inv(key, part):
    key = jax.random.fold_in(key, 2)
    key_off, key_diag = jax.random.split(key, 2)
    offdiag = jnp.clip(jax.random.normal(key_off, (NE, BLOCK, BLOCK), jnp.float32), -4.0, 4.0) * (0.6 / math.sqrt(BLOCK))
    diagonal = jax.random.uniform(key_diag, (NE, BLOCK), jnp.float32, 0.5, 1.5)
    diag_idx = jnp.arange(BLOCK)
    filled = offdiag.at[:, diag_idx, diag_idx].add(diagonal)
    return filled.astype(jnp.bfloat16)


def draw_face_nbr(key, part):
    key = jax.random.fold_in(key, 3)
    device_keys = jax.random.split(key, PEERS)

    def one_device(device_key):
        ordering = jax.random.permutation(device_key, E).astype(jnp.int32)
        struct = jnp.arange(E, dtype=jnp.int32)
        along_c = struct % ESIDE
        along_b = struct // ESIDE % ESIDE
        along_a = struct // (ESIDE * ESIDE) % ELX
        group_idx = struct // (ELX * ESIDE * ESIDE)
        slot_idx = (group_idx * ESIDE + along_b) * ESIDE + along_c

        def neighbour(a_idx, b_idx, c_idx):
            a_idx = jnp.clip(a_idx, 0, ELX - 1)
            b_idx = jnp.clip(b_idx, 0, ESIDE - 1)
            c_idx = jnp.clip(c_idx, 0, ESIDE - 1)
            return ordering[((group_idx * ELX + a_idx) * ESIDE + b_idx) * ESIDE + c_idx]
        face_cols = [jnp.where(along_a > 0, neighbour(along_a - 1, along_b, along_c), E + slot_idx), jnp.where(along_a < ELX - 1, neighbour(along_a + 1, along_b, along_c), E + IFACE + slot_idx), jnp.where(along_b > 0, neighbour(along_a, along_b - 1, along_c), -1), jnp.where(along_b < ESIDE - 1, neighbour(along_a, along_b + 1, along_c), -1), jnp.where(along_c > 0, neighbour(along_a, along_b, along_c - 1), -1), jnp.where(along_c < ESIDE - 1, neighbour(along_a, along_b, along_c + 1), -1)]
        face_rows = jnp.stack(face_cols, axis=1).astype(jnp.int32)
        return jnp.zeros((E, 6), jnp.int32).at[ordering].set(face_rows)
    return jax.vmap(one_device)(device_keys).reshape(NE, 6)


def set_ends(values, rng, least, top_value):
    longest = values.shape.index(max(values.shape))
    spots = []
    for shift in (0, 1):
        where = [jax.random.randint(jax.random.fold_in(rng, axis), (), 0, length) for axis, length in enumerate(values.shape)]
        where[longest] = (where[longest] + shift) % values.shape[longest]
        spots.append(tuple(where))
    return values.at[spots[0]].set(least).at[spots[1]].set(top_value)


def block_scale(key, shape, cuts, low, largest):
    def one(position, shards_of):
        steps = jax.random.uniform(jax.random.fold_in(jax.random.fold_in(key, 6), position), (shards_of,), jnp.float32, low / len(cuts), largest / len(cuts))
        return jnp.repeat(jnp.exp(steps), shape[position] // shards_of).reshape((-1,) + (1,) * (len(shape) - position - 1))

    level = one(*cuts[0])
    for cut in cuts[1:]:
        level = level * one(*cut)
    return level


def length_profile(number_of, total, most, skew):
    portions = [(1 << 20) // math.isqrt(standing ** skew) + 1 for standing in range(2, number_of + 1)]
    surplus, given = total - most - (number_of - 1), [1] * (number_of - 1)
    while surplus > 0:
        free = [i for i in range(number_of - 1) if given[i] < most]
        pool, left = sum([portions[i] for i in free]), surplus
        for i in free:
            addition = min(most - given[i], max(1, left * portions[i] // pool), surplus)
            given[i] = given[i] + addition
            surplus = surplus - addition
    return np.array([most] + given)


def ragged(key, count, total, limit, slope):
    if count == 2:
        one = jax.random.randint(key, (), max(1, total - limit), min(limit, total - 1) + 1)
        return jnp.stack([one, total - one])
    lengths = jnp.asarray(length_profile(count, total, limit, slope), jnp.int32)
    twos = (count - 1) // 2
    source_of, taker = lengths[1:1 + 2 * twos:2], lengths[2:2 + 2 * twos:2]
    slack = jnp.minimum(source_of - 1, limit - taker)
    passed = jax.random.randint(jax.random.fold_in(key, 1), (twos,), 0, 1 << 20) % (slack + 1)
    lengths = lengths.at[1:1 + 2 * twos:2].set(source_of - passed).at[2:2 + 2 * twos:2].set(taker + passed)
    return lengths[jax.random.permutation(jax.random.fold_in(key, 2), count)]


def shared_out(rng, own, number, rows, count, top, reach, lean):
    sequence = jax.random.permutation(rng, count)
    heavy_load, usual = load_shares(count, rows * top, reach, lean, True), load_shares(count, rows * top, reach, lean, False)
    places = jnp.arange(count)

    def named(lengths, rotation):
        used = int((lengths > 0).sum())
        fixed = max(1, used // 4)
        shifted = fixed + (places - fixed + rotation * (used - fixed)) % max(1, count - fixed)
        return jnp.zeros((count,), jnp.int32).at[sequence[jnp.where(places < fixed, places, shifted)]].set(jnp.asarray(lengths, jnp.int32))

    lengths = jnp.where(number % 4 == 0, named(heavy_load, number // 4), named(usual, number - number // 4 - 1))
    mixed = jax.random.permutation(jax.random.fold_in(own, 3), count)
    donor, sink = mixed[0:count // 2 * 2:2], mixed[1:count // 2 * 2:2]
    slack = jnp.minimum(lengths[donor] - 1, reach - lengths[sink]) // 2
    slack = jnp.where((donor == sequence[0]) | (sink == sequence[0]) | (lengths[sink] == 0), 0, jnp.maximum(slack, 0))
    shifted = jax.random.randint(jax.random.fold_in(own, 4), (count // 2,), 0, 1 << 20) % (slack + 1)
    lengths = lengths.at[donor].add(-shifted).at[sink].add(shifted)
    labels = jnp.searchsorted(jnp.cumsum(lengths), jnp.arange(rows * top), side="right").astype(jnp.int32)
    listing = labels.reshape(top, rows).T
    listing = listing[jax.random.permutation(jax.random.fold_in(own, 1), rows)]
    rotation = jax.random.randint(jax.random.fold_in(own, 2), (rows, 1), 0, top)
    return jnp.take_along_axis(listing, (jnp.arange(top)[None, :] + rotation) % top, axis=1)


def load_shares(number_of, total, most, slope, full):
    weights = [(1 << 20) // math.isqrt(standing ** slope) + 1 for standing in range(1, number_of + 1)]
    largest = most if full else min(most, max(-(-total // number_of), total * weights[0] // sum(weights)))
    least = 1 if total - largest >= number_of - 1 else 0
    given, surplus = [largest] + [least] * (number_of - 1), total - largest - least * (number_of - 1)
    while surplus > 0:
        free = [i for i in range(1, number_of) if given[i] < largest] or [i for i in range(1, number_of) if given[i] < most]
        mass, remaining = sum([weights[i] for i in free]), surplus
        for i in free:
            more = min(most - given[i], max(1, remaining * weights[i] // mass), surplus)
            given[i] = given[i] + more
            surplus = surplus - more
    return np.array(given)


def bell_draw(key, shape, scale, reach, cuts=(), kind=jnp.bfloat16):
    factor_of = block_scale(key, shape, cuts, -0.22, 0.18) if cuts else 1.0
    values = jax.random.normal(key, shape, jnp.float32) * scale * factor_of
    return jnp.minimum(jnp.maximum(values, -reach), reach).astype(kind)


def setup_inputs(seed: int = 0) -> dict:
    key_of = jax.random.split(jax.random.key(seed), 10)
    grad_rhs = draw_grad_rhs(jax.random.fold_in(key_of[9], 71), 0)
    block_inv = draw_block_inv(jax.random.fold_in(key_of[9], 71), 0)
    face_jac = bell_draw(key_of[2], (NE, 6, FACEW, FACEW), (4 * FACEW) ** -0.5, 0.3125, ((0, 128),))
    face_nbr = draw_face_nbr(jax.random.fold_in(key_of[9], 71), 0)
    recv_node = set_ends(jax.random.randint(key_of[4], (NR,), 0, E * NODES), jax.random.fold_in(key_of[4], 1), 0, (E * NODES) - 1).astype(jnp.int32)
    owners_keys = jax.random.split(jax.random.fold_in(key_of[5], 1), NR // RPTS)
    owners_turns = jax.random.permutation(jax.random.fold_in(key_of[5], 3), NR // RPTS)
    owners = jax.vmap(lambda own, number: shared_out(jax.random.fold_in(key_of[5], 2), own, number, RPTS, PEERS, 1, CAP, 2))(owners_keys, owners_turns).reshape((NR, 1))
    donor_elem = set_ends(jax.random.randint(key_of[6], (NR,), 0, E), jax.random.fold_in(key_of[6], 1), 0, E - 1).astype(jnp.int32)
    donor_coords = jnp.clip(jax.random.uniform(key_of[7], (3, NR), jnp.float32, -1.0, 1.0) * block_scale(key_of[7], (3, NR), ((1, 128),), -0.4, 0.0), -1.0, 1.0)
    recv_counts = jax.vmap(lambda own: ragged(own, NB, 96 * NB + 32, 128, 2))(jax.random.split(key_of[8], PEERS)).reshape((PEERS, NB)).astype(jnp.int32)
    return dict(grad_rhs=grad_rhs, block_inv=block_inv, face_jac=face_jac, face_nbr=face_nbr, recv_node=recv_node, owners=owners, donor_elem=donor_elem, donor_coords=donor_coords, recv_counts=recv_counts)


gll_nodes = (-1.0, -0.4472135954999579, 0.4472135954999579, 1.0)
small_eps = 1e-06

def lagrange(coord):
    factors = []
    for k in range(4):
        factor = jnp.ones_like(coord)
        for m in range(4):
            if m != k:
                factor = factor * ((coord - gll_nodes[m]) / (gll_nodes[k] - gll_nodes[m]))
        factors.append(factor)
    return jnp.stack(factors, axis=-1)

def basis_weights(coords):
    along_x = lagrange(coords[0])
    along_y = lagrange(coords[1])
    along_z = lagrange(coords[2])
    product = along_x[:, :, None, None] * along_y[:, None, :, None] * along_z[:, None, None, :]
    return product.reshape(coords.shape[1], 64)

def face_table():
    node_grid = np.arange(64).reshape(4, 4, 4)
    face_list = [node_grid[0], node_grid[3], node_grid[:, 0], node_grid[:, 3], node_grid[:, :, 0], node_grid[:, :, 3]]
    return np.stack([one_face.reshape(16) for one_face in face_list]).astype(np.int32)

def least_squares(columns, start_norm):
    count_cols = len(columns)
    cosines = []
    sine_vals = []
    rhs_vec = [start_norm] + [start_norm * 0.0 for k in range(count_cols)]
    triangle = []
    for j in range(count_cols):
        column = list(columns[j])
        for i in range(j):
            upper_one = column[i]
            lower_one = column[i + 1]
            column[i] = cosines[i] * upper_one + sine_vals[i] * lower_one
            column[i + 1] = cosines[i] * lower_one - sine_vals[i] * upper_one
        radius = jnp.sqrt(column[j] * column[j] + column[j + 1] * column[j + 1])
        cosine = column[j] / radius
        sine_val = column[j + 1] / radius
        cosines.append(cosine)
        sine_vals.append(sine_val)
        column[j] = radius
        triangle.append(column[:j + 1])
        rhs_vec[j + 1] = -sine_val * rhs_vec[j]
        rhs_vec[j] = cosine * rhs_vec[j]
    coeffs = [None] * count_cols
    for j in reversed(range(count_cols)):
        partial_val = rhs_vec[j]
        for k in range(j + 1, count_cols):
            partial_val = partial_val - triangle[k][j] * coeffs[k]
        coeffs[j] = partial_val / triangle[j][j]
    return coeffs

def adjoint_apply(vector, block_inv, face_jac, face_nbr, live_mask, source_elem, source_node, target_elem, weights):
    rounded = vector.astype(jnp.bfloat16)

    def solve_device(blocks):
        return jnp.einsum('eij,ei->ej', blocks[0].astype(jnp.float32), blocks[1].astype(jnp.float32))
    solved = lax.map(solve_device, (block_inv.reshape(PEERS, E, BLOCK, BLOCK), rounded.reshape(PEERS, E, BLOCK)))
    solved = solved.reshape(NE, BLOCK).astype(jnp.bfloat16)
    nodal_vals = solved.astype(jnp.float32).reshape(NE, VARS, NODES)
    face_nodes = face_table()
    traces = nodal_vals[:, :, face_nodes].transpose(0, 2, 1, 3).reshape(NE, 6, FACEW)

    def face_device(blocks):
        return jnp.einsum('efab,efa->efb', blocks[0].astype(jnp.float32), blocks[1])
    face_out = lax.map(face_device, (face_jac.reshape(PEERS, E, 6, FACEW, FACEW), traces.reshape(PEERS, E, 6, FACEW)))
    face_out = face_out.reshape(NE, 6, FACEW)
    device_of = jnp.arange(NE, dtype=jnp.int32)[:, None] // E
    slot_idx = jnp.where(face_nbr >= E, face_nbr - E, 2 * IFACE)
    device_rows = jnp.broadcast_to(device_of, face_nbr.shape)
    outgoing = jnp.zeros((PEERS, 2 * IFACE + 1, FACEW), jnp.float32).at[device_rows, slot_idx].add(face_out)
    outgoing = outgoing[:, :2 * IFACE].reshape(N_GRP, N_DOM, 2, IFACE, FACEW)
    from_lower = jnp.pad(outgoing[:, :-1, 1], ((0, 0), (1, 0), (0, 0), (0, 0)))
    from_upper = jnp.pad(outgoing[:, 1:, 0], ((0, 0), (0, 1), (0, 0), (0, 0)))
    arrived = jnp.stack([from_lower, from_upper], axis=2).reshape(PEERS * 2 * IFACE, FACEW)
    opposite = jnp.array([1, 0, 3, 2, 5, 4], jnp.int32)[None, :]
    local_src = (device_of * E + face_nbr) * 6 + opposite
    remote_src = NE * 6 + device_of * (2 * IFACE) + face_nbr - E
    empty_src = NE * 6 + PEERS * 2 * IFACE
    source = jnp.where(face_nbr < 0, empty_src, jnp.where(face_nbr < E, local_src, remote_src))
    trace_pool = jnp.concatenate([face_out.reshape(NE * 6, FACEW), arrived, jnp.zeros((1, FACEW), jnp.float32)])
    incoming = trace_pool[source].reshape(NE, 6, VARS, FNODES).transpose(0, 2, 1, 3)
    face_sum = jnp.zeros((NE, VARS, NODES), jnp.float32).at[:, :, face_nodes].add(incoming)
    picked = nodal_vals[source_elem, :, source_node] * live_mask[:, None]
    contrib = (picked[:, :, None] * weights[:, None, :]).reshape(NR, BLOCK)
    interp_sum = jnp.zeros((NE, BLOCK), jnp.float32).at[target_elem].add(contrib)
    return vector - face_sum.reshape(NE, BLOCK) - interp_sum

def reference(grad_rhs, block_inv, face_jac, face_nbr, recv_node, owners, donor_elem, donor_coords, recv_counts):
    point_idx = jnp.arange(NR, dtype=jnp.int32)
    device_pt = point_idx // RPTS
    within = point_idx % RPTS
    counts = recv_counts.reshape(PEERS * NB)[device_pt * NB + within // 128]
    live_mask = (within % 128 < counts).astype(jnp.float32)
    source_elem = device_pt * E + recv_node // NODES
    source_node = recv_node % NODES
    target_elem = owners[:, 0] * E + donor_elem
    weights = basis_weights(donor_coords)
    start_norm = jnp.sqrt(jnp.sum(grad_rhs * grad_rhs) + small_eps)
    krylov = [grad_rhs / start_norm]
    columns = []
    for j in range(ITERS):
        mapped = adjoint_apply(krylov[j], block_inv, face_jac, face_nbr, live_mask, source_elem, source_node, target_elem, weights)
        heights = [jnp.sum(mapped * krylov[i]) for i in range(j + 1)]
        for i in range(j + 1):
            mapped = mapped - heights[i] * krylov[i]
        length = jnp.sqrt(jnp.sum(mapped * mapped) + small_eps)
        krylov.append(mapped / length)
        columns.append(heights + [length])
    coeffs = least_squares(columns, start_norm)
    result = coeffs[0] * krylov[0]
    for j in range(1, ITERS):
        result = result + coeffs[j] * krylov[j]
    return result
```

```python
import jax
import jax.numpy as jnp
import numpy as np
from jax import lax
from jax.experimental import pallas as pl
from jax.experimental.pallas import tpu as pltpu
from jax.sharding import PartitionSpec as P

AXES = ("grp", "dom")
VARS = 5
NODES = 64
BLOCK = 320
FACEW = 80
E = 32
PEERS = 128
CAP = 8
RPTS = 512
CHUNKS = 8
SCALAR_LANE = 96
GLL = (-1.0, -0.4472135954999579, 0.4472135954999579, 1.0)
EPS = 1e-06
F32 = jnp.float32
BF16 = jnp.bfloat16
VMEM_LIMIT = 40 * 1024 * 1024


def face_table():
    grid = np.arange(64).reshape(4, 4, 4)
    faces = [grid[0], grid[3], grid[:, 0], grid[:, 3], grid[:, :, 0], grid[:, :, 3]]
    return np.stack([one.reshape(16) for one in faces])


def spread_matrix():
    table = face_table()
    out = np.zeros((6, VARS, 16, BLOCK), np.float32)
    for f in range(6):
        for v in range(VARS):
            out[f, v, np.arange(16), v * NODES + table[f]] = 1.0
    return out.reshape(6 * FACEW, BLOCK)


def dot(a, b):
    return jnp.dot(a, b, preferred_element_type=F32)


def dot_nt(a, b):
    return lax.dot_general(a, b, (((1,), (1,)), ((), ())), preferred_element_type=F32)


def dot_tn(a, b):
    return lax.dot_general(a, b, (((0,), (0,)), ((), ())), preferred_element_type=F32)


def split(x):
    hi = x.astype(BF16).astype(F32)
    return hi, x - hi


def iota(shape, dim):
    return lax.broadcasted_iota(jnp.int32, shape, dim)


def total(x):
    return jnp.sum(jnp.sum(x, axis=0, keepdims=True), axis=1, keepdims=True)


def stream(src, dst, sems):
    step = src.shape[0] // CHUNKS
    return [
        pltpu.make_async_copy(
            src.at[pl.ds(c * step, step)], dst.at[pl.ds(c * step, step)], sems.at[c]
        )
        for c in range(CHUNKS)
    ]


def block_solve(x, blocks, copies):
    step = E // CHUNKS
    row = iota((16, BLOCK), 0) % 8
    parts = []
    for g in range(E // 8):
        hi, lo = split(x[8 * g : 8 * g + 8])
        both = jnp.concatenate([hi, lo], axis=0)
        acc = None
        for k in range(8):
            e = 8 * g + k
            if e % step == 0:
                copies[e // step].wait()
            one = dot(jnp.where(row == k, both, 0.0).astype(BF16), blocks[e])
            acc = one if acc is None else acc + one
        parts.append(acc[:8] + acc[8:])
    return jnp.concatenate(parts, axis=0)


def pick(z, recv_node, counts):
    hi, lo = split(z)
    rows = [part[:, v * NODES : (v + 1) * NODES] for part in (hi, lo) for v in range(VARS)]
    rows = jnp.concatenate(rows, axis=0).astype(BF16)
    elem = lax.shift_right_logical(recv_node, 6)
    node = jnp.bitwise_and(recv_node, NODES - 1)
    node_hot = (iota((NODES, RPTS), 0) == node).astype(F32).astype(BF16)
    at_node = dot(rows, node_hot)
    at_node = at_node[: VARS * E] + at_node[VARS * E :]
    lane = iota((1, RPTS), 1)
    block = lax.shift_right_logical(lane, 7)
    count = jnp.where(
        block == 0, counts[0], jnp.where(block == 1, counts[1], jnp.where(block == 2, counts[2], counts[3]))
    )
    live = jnp.bitwise_and(lane, 127) < count
    elem = jnp.where(live, elem, -1)
    elem_hot = iota((E, RPTS), 0) == elem
    return [
        jnp.sum(jnp.where(elem_hot, at_node[v * E : (v + 1) * E], 0.0), axis=0, keepdims=True)
        for v in range(VARS)
    ]


def pack(owner_hot, rank, comps):
    slot = iota((CAP, RPTS), 0) == rank
    rows = [jnp.where(slot, comp, 0.0) for comp in comps]
    rows.append(jnp.zeros((PEERS - CAP * len(comps), RPTS), F32))
    rows = jnp.concatenate(rows, axis=0)
    hi, rest = split(rows)
    mid, low = split(rest)
    out = dot_nt(owner_hot, jnp.concatenate([hi, mid, low], axis=0).astype(BF16))
    return (out[:, :PEERS] + out[:, PEERS : 2 * PEERS]) + out[:, 2 * PEERS :]


def owner_one_hot(owners):
    return (iota((PEERS, RPTS), 0) == owners).astype(F32)


def lagrange(coord):
    factors = []
    for k in range(4):
        factor = None
        for m in range(4):
            if m != k:
                one = (coord - GLL[m]) * (1.0 / (GLL[k] - GLL[m]))
                factor = one if factor is None else factor * one
        factors.append(factor)
    return factors


def interpolate(values, geometry, table):
    values = values.T
    geometry = geometry.T
    val = [values[8 * c : 8 * c + 8] for c in range(VARS)]
    parts = [split(one) for one in val]
    coords = [geometry[8 * (VARS + c) : 8 * (VARS + c) + 8] for c in range(3)]
    rows = [one for coord in coords for one in lagrange(coord)]
    rows.append(geometry[8 * (VARS + 3) : 8 * (VARS + 3) + 8])
    rows += [part[0] for part in parts] + [part[1] for part in parts]
    for c, one in enumerate(rows):
        table[8 * c : 8 * c + 8, :] = one
    sub = iota((8, PEERS), 0)
    elem_id = iota((E, PEERS), 0).astype(F32)
    left = []
    right = []
    for k in range(CAP):

        def row(c):
            return table[pl.ds(8 * c + k, 1), :]

        inner = sub % 4
        along_z = jnp.where(
            inner == 0, row(8), jnp.where(inner == 1, row(9), jnp.where(inner == 2, row(10), row(11)))
        )
        lower = jnp.where(sub < 4, row(4), row(5)) * along_z
        upper = jnp.where(sub < 4, row(6), row(7)) * along_z
        basis = jnp.concatenate(
            [half * row(i) for i in range(4) for half in (lower, upper)], axis=0
        )
        hi, lo = split(basis)
        right.append(jnp.concatenate([hi, lo], axis=0).astype(BF16))
        mask = elem_id == row(12)
        left.append(
            jnp.concatenate(
                [jnp.where(mask, row(13 + c), 0.0) for c in range(2 * VARS)], axis=0
            ).astype(BF16)
        )
    out = dot_nt(jnp.concatenate(left, axis=1), jnp.concatenate(right, axis=1))
    half = VARS * E
    out = out[:half, :NODES] + (out[:half, NODES:] + out[half:, :NODES])
    return jnp.concatenate([out[v * E : (v + 1) * E] for v in range(VARS)], axis=1)


def first_kernel(
    x_ref, blocks_ref, node_ref, owner_ref, elem_ref, coord_ref, count_ref,
    z_ref, pay_ref, rank_ref, buf, sems,
):
    copies = stream(blocks_ref, buf, sems)
    for one in copies:
        one.start()
    hot = owner_one_hot(owner_ref[...])
    hot16 = hot.astype(BF16)
    earlier = (iota((RPTS, RPTS), 0) < iota((RPTS, RPTS), 1)).astype(F32).astype(BF16)
    rank = jnp.sum(hot * dot(hot16, earlier), axis=0, keepdims=True).astype(jnp.int32)
    rank_ref[...] = rank
    z = block_solve(x_ref[...], buf, copies)
    z_ref[...] = z
    counts = [count_ref[0, i] for i in range(4)]
    comps = pick(z, node_ref[...], counts)
    comps += [coord_ref[c : c + 1, :] for c in range(3)]
    comps.append(elem_ref[...].astype(F32))
    pay_ref[...] = pack(hot16, rank, comps)


def face_kernel(
    z_ref, x_ref, jac_ref, nbr_ref, spread_ref,
    base_ref, low_ref, high_ref, traces, outs, buf, sems,
):
    copies = stream(jac_ref, buf, sems)
    for one in copies:
        one.start()
    hi, lo = split(z_ref[...])
    traces[...] = dot_nt(jnp.concatenate([hi, lo], axis=0).astype(BF16), spread_ref[...])
    own_face = iota((16, 6 * FACEW), 1) // FACEW == iota((16, 6 * FACEW), 0) % 8
    step = E // CHUNKS
    for e in range(E):
        if e % step == 0:
            copies[e // step].wait()
        both = jnp.concatenate(
            [
                jnp.broadcast_to(traces[pl.ds(e, 1), :], (8, 6 * FACEW)),
                jnp.broadcast_to(traces[pl.ds(E + e, 1), :], (8, 6 * FACEW)),
            ],
            axis=0,
        )
        one = dot(jnp.where(own_face, both, 0.0).astype(BF16), buf[e])
        outs[8 * e : 8 * e + 8, 0:FACEW] = one[:8] + one[8:]
    out = jnp.concatenate(
        [outs[pl.ds(f, E, stride=8), :][:, :FACEW] for f in range(6)], axis=0
    )
    hi, lo = split(out)
    hi, lo = hi.astype(BF16), lo.astype(BF16)
    local_hot, iface_hot = neighbour_one_hots(nbr_ref[...])
    outgoing = dot(iface_hot, hi) + dot(iface_hot, lo)
    low_ref[...] = outgoing[:E]
    high_ref[...] = outgoing[E:]
    incoming = dot_tn(local_hot, hi) + dot_tn(local_hot, lo)
    base_ref[...] = x_ref[...] - spread_faces(incoming, spread_ref)


def neighbour_one_hots(nbr):
    target = jnp.concatenate(
        [
            jnp.where(nbr[f : f + 1] < 0, -1, jnp.where(nbr[f : f + 1] < E, nbr[f : f + 1] + (f ^ 1) * E, nbr[f : f + 1] + 5 * E))
            for f in range(6)
        ],
        axis=1,
    )
    hot = (iota((8 * E, 6 * E), 0) == target).astype(F32).astype(BF16)
    return hot[: 6 * E], hot[6 * E :]


def spread_faces(incoming, spread_ref):
    hi, lo = split(incoming)
    acc = None
    for f in range(6):
        both = jnp.concatenate([hi[f * E : (f + 1) * E], lo[f * E : (f + 1) * E]], axis=0)
        one = dot(both.astype(BF16), spread_ref[f * FACEW : (f + 1) * FACEW, :])
        acc = one if acc is None else acc + one
    return acc[:E] + acc[E:]


def arrived_kernel(base_ref, low_ref, high_ref, nbr_ref, spread_ref, out_ref):
    hi, lo = split(jnp.concatenate([low_ref[...], high_ref[...]], axis=0))
    _, iface_hot = neighbour_one_hots(nbr_ref[...])
    incoming = dot_tn(iface_hot, hi.astype(BF16)) + dot_tn(iface_hot, lo.astype(BF16))
    out_ref[...] = base_ref[...] - spread_faces(incoming, spread_ref)


def with_scalars(table, scalars):
    lane = iota(table.shape, 1)
    for i, one in enumerate(scalars):
        table = jnp.where(lane == SCALAR_LANE + i, one, table)
    return table


def read_scalars(table, count):
    row = jnp.sum(table, axis=0, keepdims=True)
    return [row[:, SCALAR_LANE + i : SCALAR_LANE + i + 1] for i in range(count)]


def second_kernel(
    base_ref, got_ref, b_ref, blocks_ref, node_ref, owner_ref, rank_ref, count_ref,
    u_ref, z_ref, pay_ref, table, buf, sems,
):
    copies = stream(blocks_ref, buf, sems)
    for one in copies:
        one.start()
    got = got_ref[...]
    u = base_ref[...] - interpolate(got, got, table)
    u_ref[...] = u
    b = b_ref[...]
    z = block_solve(u, buf, copies)
    z_ref[...] = z
    counts = [count_ref[0, i] for i in range(4)]
    comps = pick(z, node_ref[...], counts)
    hot = owner_one_hot(owner_ref[...]).astype(BF16)
    pay = pack(hot, rank_ref[...], comps)
    pay_ref[...] = with_scalars(pay, [total(b * b), total(b * u)])


def third_kernel(base_ref, got_ref, first_ref, b_ref, u_ref, rest_ref, pay_ref, known_ref, table):
    got = got_ref[...]
    w = base_ref[...] - interpolate(got, first_ref[...], table)
    bb, bu = read_scalars(got, 2)
    h00 = bu / (bb + EPS)
    b = b_ref[...]
    u = u_ref[...]
    rest = u - h00 * b
    mapped = w - h00 * u
    rest_ref[...] = rest
    scalars = [
        total(rest * rest), total(b * rest), total(mapped * b), total(mapped * rest), total(mapped * mapped),
    ]
    pay_ref[...] = with_scalars(jnp.zeros((PEERS, PEERS), F32), scalars)
    known_ref[...] = with_scalars(jnp.zeros((8, PEERS), F32), [bb * 0.125, bu * 0.125])


def last_kernel(got_ref, known_ref, b_ref, rest_ref, out_ref):
    bb, bu = read_scalars(known_ref[...], 2)
    rr, br, mb, mr, mm = read_scalars(got_ref[...], 5)
    s2 = bb + EPS
    start = jnp.sqrt(s2)
    h00 = bu / s2
    h10 = jnp.sqrt(rr / s2 + EPS)
    h01 = mb / (s2 * h10)
    scale = s2 * (h10 * h10)
    h11 = mr / scale
    left = (
        mm / scale
        - h01 * h01 * (2.0 - bb / s2)
        - h11 * h11 * (2.0 - rr / scale)
        + 2.0 * h01 * h11 * (br / (s2 * h10))
    )
    h21 = jnp.sqrt(jnp.maximum(left, 0.0) + EPS)
    r00 = jnp.sqrt(h00 * h00 + h10 * h10)
    c0 = h00 / r00
    s0 = h10 / r00
    r01 = c0 * h01 + s0 * h11
    low = c0 * h11 - s0 * h01
    r11 = jnp.sqrt(low * low + h21 * h21)
    c1 = low / r11
    y1 = c1 * (-s0 * start) / r11
    y0 = (c0 * start - r01 * y1) / r00
    out_ref[...] = (y0 / start) * b_ref[...] + (y1 / (start * h10)) * rest_ref[...]


VM = pl.BlockSpec(memory_space=pltpu.VMEM)
SM = pl.BlockSpec(memory_space=pltpu.SMEM)
ANY = pl.BlockSpec(memory_space=pl.ANY)


def call(kernel, in_specs, outs, scratch, *args):
    return pl.pallas_call(
        kernel,
        in_specs=in_specs,
        out_specs=[VM] * len(outs),
        out_shape=[jax.ShapeDtypeStruct(shape, dtype) for shape, dtype in outs],
        scratch_shapes=scratch,
        compiler_params=pltpu.CompilerParams(vmem_limit_bytes=VMEM_LIMIT),
        name=kernel.__name__,
    )(*args)


def exchange(table):
    return lax.all_to_all(
        table.reshape(PEERS, 1, PEERS), AXES, split_axis=0, concat_axis=0, tiled=True
    ).reshape(PEERS, PEERS)


def local(
    grad_rhs, block_inv, face_jac, face_nbr, recv_node, owners, donor_elem, donor_coords, recv_counts
):
    jac = face_jac.reshape(E, 6 * FACEW, FACEW)
    nbr = face_nbr.T
    node = recv_node.reshape(1, RPTS)
    owner = owners.reshape(1, RPTS)
    elem = donor_elem.reshape(1, RPTS)
    spread = jnp.asarray(spread_matrix(), BF16)
    ends = lax.axis_size("dom") - 1
    upward = [(i, i + 1) for i in range(ends)]
    downward = [(i + 1, i) for i in range(ends)]
    full = ((E, BLOCK), F32)
    table = ((PEERS, PEERS), F32)
    half = ((E, FACEW), F32)
    block_scratch = [pltpu.VMEM((E, BLOCK, BLOCK), BF16), pltpu.SemaphoreType.DMA((CHUNKS,))]
    rows_scratch = pltpu.VMEM((8 * (13 + 2 * VARS), PEERS), F32)

    def faces(z, x):
        base, low, high = call(
            face_kernel,
            [VM, VM, ANY, VM, VM],
            [full, half, half],
            [
                pltpu.VMEM((2 * E, 6 * FACEW), F32),
                pltpu.VMEM((8 * E, PEERS), F32),
                pltpu.VMEM((E, 6 * FACEW, FACEW), BF16),
                pltpu.SemaphoreType.DMA((CHUNKS,)),
            ],
            z, x, jac, nbr, spread,
        )
        from_lower = lax.ppermute(high, "dom", upward)
        from_upper = lax.ppermute(low, "dom", downward)
        return call(
            arrived_kernel, [VM] * 5, [full], [], base, from_lower, from_upper, nbr, spread
        )[0]

    z1, pay1, rank = call(
        first_kernel,
        [VM, ANY, VM, VM, VM, VM, SM],
        [full, table, ((1, RPTS), jnp.int32)],
        block_scratch,
        grad_rhs, block_inv, node, owner, elem, donor_coords, recv_counts,
    )
    got1 = exchange(pay1)
    base1 = faces(z1, grad_rhs)
    u, z2, pay2 = call(
        second_kernel,
        [VM, VM, VM, ANY, VM, VM, VM, SM],
        [full, full, table],
        [rows_scratch] + block_scratch,
        base1, got1, grad_rhs, block_inv, node, owner, rank, recv_counts,
    )
    got2 = exchange(pay2)
    base2 = faces(z2, u)
    rest, pay3, known = call(
        third_kernel,
        [VM] * 5,
        [full, table, ((8, PEERS), F32)],
        [rows_scratch],
        base2, got2, got1, grad_rhs, u,
    )
    got3 = exchange(pay3)
    return call(last_kernel, [VM] * 4, [full], [], got3, known, grad_rhs, rest)[0]


def solution(mesh):
    placed = (
        P(AXES, None),
        P(AXES, None, None),
        P(AXES, None, None, None),
        P(AXES, None),
        P(AXES),
        P(AXES, None),
        P(AXES),
        P(None, AXES),
        P(AXES, None),
    )
    return jax.shard_map(
        local, mesh=mesh, in_specs=placed, out_specs=P(AXES, None), check_vma=False
    )
```

```python
import jax
import jax.numpy as jnp
import numpy as np
from jax import lax
from jax.experimental import pallas as pl
from jax.experimental.pallas import tpu as pltpu
from jax.sharding import PartitionSpec as P

AXES = ("grp", "dom")
VARS = 5
NODES = 64
BLOCK = 320
FACEW = 80
E = 32
PEERS = 128
CAP = 8
RPTS = 512
CHUNKS = 8
SCALAR_LANE = 96
GLL = (-1.0, -0.4472135954999579, 0.4472135954999579, 1.0)
EPS = 1e-06
F32 = jnp.float32
BF16 = jnp.bfloat16
VMEM_LIMIT = 24 * 1024 * 1024


def face_table():
    grid = np.arange(64).reshape(4, 4, 4)
    faces = [grid[0], grid[3], grid[:, 0], grid[:, 3], grid[:, :, 0], grid[:, :, 3]]
    return np.stack([one.reshape(16) for one in faces])


def spread_matrix():
    table = face_table()
    out = np.zeros((6, VARS, 16, BLOCK), np.float32)
    for f in range(6):
        for v in range(VARS):
            out[f, v, np.arange(16), v * NODES + table[f]] = 1.0
    return out.reshape(6 * FACEW, BLOCK)


def dot(a, b):
    return jnp.dot(a, b, preferred_element_type=F32)


def dot_nt(a, b):
    return lax.dot_general(a, b, (((1,), (1,)), ((), ())), preferred_element_type=F32)


def dot_tn(a, b):
    return lax.dot_general(a, b, (((0,), (0,)), ((), ())), preferred_element_type=F32)


def split(x):
    hi = x.astype(BF16).astype(F32)
    return hi, x - hi


def iota(shape, dim):
    return lax.broadcasted_iota(jnp.int32, shape, dim)


def total(x):
    return jnp.sum(jnp.sum(x, axis=0, keepdims=True), axis=1, keepdims=True)


def stream(src, dst, sems):
    step = src.shape[0] // CHUNKS
    return [
        pltpu.make_async_copy(
            src.at[pl.ds(c * step, step)], dst.at[pl.ds(c * step, step)], sems.at[c]
        )
        for c in range(CHUNKS)
    ]


def block_solve(x, blocks, copies):
    step = E // CHUNKS
    row = iota((16, BLOCK), 0) % 8
    parts = []
    for g in range(E // 8):
        hi, lo = split(x[8 * g : 8 * g + 8])
        both = jnp.concatenate([hi, lo], axis=0)
        acc = None
        for k in range(8):
            e = 8 * g + k
            if e % step == 0:
                copies[e // step].wait()
            one = dot(jnp.where(row == k, both, 0.0).astype(BF16), blocks[e])
            acc = one if acc is None else acc + one
        parts.append(acc[:8] + acc[8:])
    return jnp.concatenate(parts, axis=0)


def pick(z, recv_node, counts):
    hi, lo = split(z)
    rows = [part[:, v * NODES : (v + 1) * NODES] for part in (hi, lo) for v in range(VARS)]
    rows = jnp.concatenate(rows, axis=0).astype(BF16)
    elem = lax.shift_right_logical(recv_node, 6)
    node = jnp.bitwise_and(recv_node, NODES - 1)
    node_hot = (iota((NODES, RPTS), 0) == node).astype(F32).astype(BF16)
    at_node = dot(rows, node_hot)
    at_node = at_node[: VARS * E] + at_node[VARS * E :]
    lane = iota((1, RPTS), 1)
    block = lax.shift_right_logical(lane, 7)
    count = jnp.where(
        block == 0, counts[0], jnp.where(block == 1, counts[1], jnp.where(block == 2, counts[2], counts[3]))
    )
    live = jnp.bitwise_and(lane, 127) < count
    elem = jnp.where(live, elem, -1)
    elem_hot = iota((E, RPTS), 0) == elem
    return [
        jnp.sum(jnp.where(elem_hot, at_node[v * E : (v + 1) * E], 0.0), axis=0, keepdims=True)
        for v in range(VARS)
    ]


def pack(owner_hot, rank, comps):
    slot = iota((CAP, RPTS), 0) == rank
    rows = [jnp.where(slot, comp, 0.0) for comp in comps]
    rows.append(jnp.zeros((PEERS - CAP * len(comps), RPTS), F32))
    rows = jnp.concatenate(rows, axis=0)
    hi, rest = split(rows)
    mid, low = split(rest)
    out = dot_nt(owner_hot, jnp.concatenate([hi, mid, low], axis=0).astype(BF16))
    return (out[:, :PEERS] + out[:, PEERS : 2 * PEERS]) + out[:, 2 * PEERS :]


def owner_one_hot(owners):
    return (iota((PEERS, RPTS), 0) == owners).astype(F32)


def lagrange(coord):
    factors = []
    for k in range(4):
        factor = None
        for m in range(4):
            if m != k:
                one = (coord - GLL[m]) * (1.0 / (GLL[k] - GLL[m]))
                factor = one if factor is None else factor * one
        factors.append(factor)
    return factors


def interpolate(values, geometry, table):
    values = values.T
    geometry = geometry.T
    val = [values[8 * c : 8 * c + 8] for c in range(VARS)]
    parts = [split(one) for one in val]
    coords = [geometry[8 * (VARS + c) : 8 * (VARS + c) + 8] for c in range(3)]
    rows = [one for coord in coords for one in lagrange(coord)]
    rows.append(geometry[8 * (VARS + 3) : 8 * (VARS + 3) + 8])
    rows += [part[0] for part in parts] + [part[1] for part in parts]
    for c, one in enumerate(rows):
        table[8 * c : 8 * c + 8, :] = one
    sub = iota((8, PEERS), 0)
    elem_id = iota((E, PEERS), 0).astype(F32)
    left = []
    right = []
    for k in range(CAP):

        def row(c):
            return table[pl.ds(8 * c + k, 1), :]

        inner = sub % 4
        along_z = jnp.where(
            inner == 0, row(8), jnp.where(inner == 1, row(9), jnp.where(inner == 2, row(10), row(11)))
        )
        lower = jnp.where(sub < 4, row(4), row(5)) * along_z
        upper = jnp.where(sub < 4, row(6), row(7)) * along_z
        basis = jnp.concatenate(
            [half * row(i) for i in range(4) for half in (lower, upper)], axis=0
        )
        hi, lo = split(basis)
        right.append(jnp.concatenate([hi, lo], axis=0).astype(BF16))
        mask = elem_id == row(12)
        left.append(
            jnp.concatenate(
                [jnp.where(mask, row(13 + c), 0.0) for c in range(2 * VARS)], axis=0
            ).astype(BF16)
        )
    out = dot_nt(jnp.concatenate(left, axis=1), jnp.concatenate(right, axis=1))
    half = VARS * E
    out = out[:half, :NODES] + (out[:half, NODES:] + out[half:, :NODES])
    return jnp.concatenate([out[v * E : (v + 1) * E] for v in range(VARS)], axis=1)


def first_kernel(
    x_hbm, blocks_ref, node_hbm, owner_hbm, elem_hbm, coord_hbm, count_hbm,
    z_ref, pay_ref, rank_ref,
    x_ref, node_ref, owner_ref, elem_ref, coord_ref, count_ref, small_sems, buf, sems,
):
    small = [
        pltpu.make_async_copy(src, dst, small_sems.at[i])
        for i, (src, dst) in enumerate(
            [
                (owner_hbm, owner_ref), (x_hbm, x_ref), (node_hbm, node_ref),
                (elem_hbm, elem_ref), (coord_hbm, coord_ref), (count_hbm, count_ref),
            ]
        )
    ]
    copies = stream(blocks_ref, buf, sems)
    for one in small + copies:
        one.start()
    for one in small:
        one.wait()
    hot = owner_one_hot(owner_ref[...])
    hot16 = hot.astype(BF16)
    earlier = (iota((RPTS, RPTS), 0) < iota((RPTS, RPTS), 1)).astype(F32).astype(BF16)
    rank = jnp.sum(hot * dot(hot16, earlier), axis=0, keepdims=True).astype(jnp.int32)
    rank_ref[...] = rank
    z = block_solve(x_ref[...], buf, copies)
    z_ref[...] = z
    counts = [count_ref[0, i] for i in range(4)]
    comps = pick(z, node_ref[...], counts)
    comps += [coord_ref[c : c + 1, :] for c in range(3)]
    comps.append(elem_ref[...].astype(F32))
    pay_ref[...] = pack(hot16, rank, comps)


def face_kernel(
    z_ref, x_ref, jac_ref, nbr_ref, spread_ref,
    base_ref, first_ref, second_ref, traces, outs, buf, sems,
):
    copies = stream(jac_ref, buf, sems)
    for one in copies:
        one.start()
    hi, lo = split(z_ref[...])
    traces[...] = dot_nt(jnp.concatenate([hi, lo], axis=0).astype(BF16), spread_ref[...])
    own_face = iota((16, 6 * FACEW), 1) // FACEW == iota((16, 6 * FACEW), 0) % 8
    step = E // CHUNKS
    for e in range(E):
        if e % step == 0:
            copies[e // step].wait()
        both = jnp.concatenate(
            [
                jnp.broadcast_to(traces[pl.ds(e, 1), :], (8, 6 * FACEW)),
                jnp.broadcast_to(traces[pl.ds(E + e, 1), :], (8, 6 * FACEW)),
            ],
            axis=0,
        )
        one = dot(jnp.where(own_face, both, 0.0).astype(BF16), buf[e])
        outs[8 * e : 8 * e + 8, 0:FACEW] = one[:8] + one[8:]
    out = jnp.concatenate(
        [outs[pl.ds(f, E, stride=8), :][:, :FACEW] for f in range(6)], axis=0
    )
    hi, lo = split(out)
    hi, lo = hi.astype(BF16), lo.astype(BF16)
    local_hot, iface_hot = neighbour_one_hots(nbr_ref[...])
    outgoing = dot(iface_hot, hi) + dot(iface_hot, lo)
    odd = lax.axis_index("dom") % 2 == 1
    low, high = outgoing[:E], outgoing[E:]
    first_ref[...] = jnp.where(odd, low, high)
    second_ref[...] = jnp.where(odd, high, low)
    incoming = dot_tn(local_hot, hi) + dot_tn(local_hot, lo)
    base_ref[...] = x_ref[...] - spread_faces(incoming, spread_ref)


def neighbour_one_hots(nbr):
    target = jnp.concatenate(
        [
            jnp.where(nbr[f : f + 1] < 0, -1, jnp.where(nbr[f : f + 1] < E, nbr[f : f + 1] + (f ^ 1) * E, nbr[f : f + 1] + 5 * E))
            for f in range(6)
        ],
        axis=1,
    )
    hot = (iota((8 * E, 6 * E), 0) == target).astype(F32).astype(BF16)
    return hot[: 6 * E], hot[6 * E :]


def spread_faces(incoming, spread_ref):
    hi, lo = split(incoming)
    acc = None
    for f in range(6):
        both = jnp.concatenate([hi[f * E : (f + 1) * E], lo[f * E : (f + 1) * E]], axis=0)
        one = dot(both.astype(BF16), spread_ref[f * FACEW : (f + 1) * FACEW, :])
        acc = one if acc is None else acc + one
    return acc[:E] + acc[E:]


def arrived_kernel(base_ref, first_ref, second_ref, nbr_ref, spread_ref, out_ref):
    odd = lax.axis_index("dom") % 2 == 1
    first, second = first_ref[...], second_ref[...]
    low, high = jnp.where(odd, first, second), jnp.where(odd, second, first)
    hi, lo = split(jnp.concatenate([low, high], axis=0))
    _, iface_hot = neighbour_one_hots(nbr_ref[...])
    incoming = dot_tn(iface_hot, hi.astype(BF16)) + dot_tn(iface_hot, lo.astype(BF16))
    out_ref[...] = base_ref[...] - spread_faces(incoming, spread_ref)


def with_scalars(table, scalars):
    lane = iota(table.shape, 1)
    for i, one in enumerate(scalars):
        table = jnp.where(lane == SCALAR_LANE + i, one, table)
    return table


def read_scalars(table, count):
    row = jnp.sum(table, axis=0, keepdims=True)
    return [row[:, SCALAR_LANE + i : SCALAR_LANE + i + 1] for i in range(count)]


def second_kernel(
    base_ref, got_ref, b_ref, blocks_ref, node_ref, owner_ref, rank_ref, count_ref,
    u_ref, z_ref, pay_ref, table, buf, sems,
):
    copies = stream(blocks_ref, buf, sems)
    for one in copies:
        one.start()
    got = got_ref[...]
    u = base_ref[...] - interpolate(got, got, table)
    u_ref[...] = u
    b = b_ref[...]
    z = block_solve(u, buf, copies)
    z_ref[...] = z
    counts = [count_ref[0, i] for i in range(4)]
    comps = pick(z, node_ref[...], counts)
    hot = owner_one_hot(owner_ref[...]).astype(BF16)
    pay = pack(hot, rank_ref[...], comps)
    pay_ref[...] = with_scalars(pay, [total(b * b), total(b * u)])


def third_kernel(base_ref, got_ref, first_ref, b_ref, u_ref, rest_ref, pay_ref, known_ref, table):
    got = got_ref[...]
    w = base_ref[...] - interpolate(got, first_ref[...], table)
    bb, bu = read_scalars(got, 2)
    h00 = bu / (bb + EPS)
    b = b_ref[...]
    u = u_ref[...]
    rest = u - h00 * b
    mapped = w - h00 * u
    rest_ref[...] = rest
    scalars = [
        total(rest * rest), total(b * rest), total(mapped * b), total(mapped * rest), total(mapped * mapped),
    ]
    pay_ref[...] = with_scalars(jnp.zeros((PEERS, PEERS), F32), scalars)
    known_ref[...] = with_scalars(jnp.zeros((8, PEERS), F32), [bb * 0.125, bu * 0.125])


def last_kernel(got_ref, known_ref, b_ref, rest_ref, out_ref):
    bb, bu = read_scalars(known_ref[...], 2)
    rr, br, mb, mr, mm = read_scalars(got_ref[...], 5)
    s2 = bb + EPS
    start = jnp.sqrt(s2)
    h00 = bu / s2
    h10 = jnp.sqrt(rr / s2 + EPS)
    h01 = mb / (s2 * h10)
    scale = s2 * (h10 * h10)
    h11 = mr / scale
    left = (
        mm / scale
        - h01 * h01 * (2.0 - bb / s2)
        - h11 * h11 * (2.0 - rr / scale)
        + 2.0 * h01 * h11 * (br / (s2 * h10))
    )
    h21 = jnp.sqrt(jnp.maximum(left, 0.0) + EPS)
    r00 = jnp.sqrt(h00 * h00 + h10 * h10)
    c0 = h00 / r00
    s0 = h10 / r00
    r01 = c0 * h01 + s0 * h11
    low = c0 * h11 - s0 * h01
    r11 = jnp.sqrt(low * low + h21 * h21)
    c1 = low / r11
    y1 = c1 * (-s0 * start) / r11
    y0 = (c0 * start - r01 * y1) / r00
    out_ref[...] = (y0 / start) * b_ref[...] + (y1 / (start * h10)) * rest_ref[...]


VM = pl.BlockSpec(memory_space=pltpu.VMEM)
SM = pl.BlockSpec(memory_space=pltpu.SMEM)


HBM = pl.BlockSpec(memory_space=pltpu.HBM)


def swaps(start, ends):
    return [pair for i in range(start, ends, 2) for pair in ((i, i + 1), (i + 1, i))]


def in_hbm(x):
    return pltpu.with_memory_space_constraint(x, pltpu.HBM)


def call(kernel, in_specs, outs, scratch, *args):
    return pl.pallas_call(
        kernel,
        in_specs=in_specs,
        out_specs=[VM] * len(outs),
        out_shape=[jax.ShapeDtypeStruct(shape, dtype) for shape, dtype in outs],
        scratch_shapes=scratch,
        compiler_params=pltpu.CompilerParams(vmem_limit_bytes=VMEM_LIMIT),
        name=kernel.__name__,
    )(*args)


def exchange(table):
    return lax.all_to_all(
        table.reshape(PEERS, 1, PEERS), AXES, split_axis=0, concat_axis=0, tiled=True
    ).reshape(PEERS, PEERS)


def local(
    grad_rhs, block_inv, face_jac, face_nbr, recv_node, owners, donor_elem, donor_coords, recv_counts
):
    jac = face_jac.reshape(E, 6 * FACEW, FACEW)
    nbr = face_nbr.T
    node = recv_node.reshape(1, RPTS)
    owner = owners.reshape(1, RPTS)
    elem = donor_elem.reshape(1, RPTS)
    spread = jnp.asarray(spread_matrix(), BF16)
    ends = lax.axis_size("dom") - 1
    even_pairs = swaps(0, ends)
    odd_pairs = swaps(1, ends)
    full = ((E, BLOCK), F32)
    table = ((PEERS, PEERS), F32)
    half = ((E, FACEW), F32)
    row = pltpu.VMEM((1, RPTS), jnp.int32)
    block_scratch = [pltpu.VMEM((E, BLOCK, BLOCK), BF16), pltpu.SemaphoreType.DMA((CHUNKS,))]
    blocks = in_hbm(block_inv)
    jac = in_hbm(jac)
    rows_scratch = pltpu.VMEM((8 * (13 + 2 * VARS), PEERS), F32)

    def faces(z, x):
        base, first, second = call(
            face_kernel,
            [VM, VM, HBM, VM, VM],
            [full, half, half],
            [
                pltpu.VMEM((2 * E, 6 * FACEW), F32),
                pltpu.VMEM((8 * E, PEERS), F32),
                pltpu.VMEM((E, 6 * FACEW, FACEW), BF16),
                pltpu.SemaphoreType.DMA((CHUNKS,)),
            ],
            z, x, jac, nbr, spread,
        )
        second = lax.ppermute(second, "dom", odd_pairs)
        first = lax.ppermute(first, "dom", even_pairs)
        return call(arrived_kernel, [VM] * 5, [full], [], base, first, second, nbr, spread)[0]

    z1, pay1, rank = call(
        first_kernel,
        [HBM] * 7,
        [full, table, ((1, RPTS), jnp.int32)],
        [
            pltpu.VMEM((E, BLOCK), F32), row, row, row, pltpu.VMEM((3, RPTS), F32),
            pltpu.SMEM((1, 4), jnp.int32),
            pltpu.SemaphoreType.DMA((6,)),
        ]
        + block_scratch,
        in_hbm(grad_rhs), blocks, in_hbm(node), in_hbm(owner), in_hbm(elem),
        in_hbm(donor_coords), in_hbm(recv_counts),
    )
    got1 = exchange(pay1)
    base1 = faces(z1, grad_rhs)
    u, z2, pay2 = call(
        second_kernel,
        [VM, VM, VM, HBM, VM, VM, VM, SM],
        [full, full, table],
        [rows_scratch] + block_scratch,
        base1, got1, grad_rhs, blocks, node, owner, rank, recv_counts,
    )
    got2 = exchange(pay2)
    base2 = faces(z2, u)
    rest, pay3, known = call(
        third_kernel,
        [VM] * 5,
        [full, table, ((8, PEERS), F32)],
        [rows_scratch],
        base2, got2, got1, grad_rhs, u,
    )
    got3 = exchange(pay3)
    return call(last_kernel, [VM] * 4, [full], [], got3, known, grad_rhs, rest)[0]


def solution(mesh):
    placed = (
        P(AXES, None),
        P(AXES, None, None),
        P(AXES, None, None, None),
        P(AXES, None),
        P(AXES),
        P(AXES, None),
        P(AXES),
        P(None, AXES),
        P(AXES, None),
    )
    return jax.shard_map(
        local, mesh=mesh, in_specs=placed, out_specs=P(AXES, None), check_vma=False
    )
```

```python
import jax
import jax.numpy as jnp
import numpy as np
from jax import lax
from jax.experimental import pallas as pl
from jax.experimental.pallas import tpu as pltpu
from jax.sharding import PartitionSpec as P

AXES = ("grp", "dom")
VARS = 5
NODES = 64
BLOCK = 320
FACEW = 80
E = 32
PEERS = 128
CAP = 8
RPTS = 512
BLOCK_CHUNKS = (16, 16)
START_JAC = 0
AHEAD = 2
JAC_CHUNKS = (16, 16)
SCALAR_LANE = 96
GLL = (-1.0, -0.4472135954999579, 0.4472135954999579, 1.0)
EPS = 1e-06
F32 = jnp.float32
BF16 = jnp.bfloat16
VMEM_LIMIT = 24 * 1024 * 1024


def face_table():
    grid = np.arange(64).reshape(4, 4, 4)
    faces = [grid[0], grid[3], grid[:, 0], grid[:, 3], grid[:, :, 0], grid[:, :, 3]]
    return np.stack([one.reshape(16) for one in faces])


def spread_matrix():
    table = face_table()
    out = np.zeros((6, VARS, 16, BLOCK), np.float32)
    for f in range(6):
        for v in range(VARS):
            out[f, v, np.arange(16), v * NODES + table[f]] = 1.0
    return out.reshape(6 * FACEW, BLOCK)


def dot(a, b):
    return jnp.dot(a, b, preferred_element_type=F32)


def dot_nt(a, b):
    return lax.dot_general(a, b, (((1,), (1,)), ((), ())), preferred_element_type=F32)


def dot_tn(a, b):
    return lax.dot_general(a, b, (((0,), (0,)), ((), ())), preferred_element_type=F32)


def split(x):
    hi = x.astype(BF16).astype(F32)
    return hi, x - hi


def iota(shape, dim):
    return lax.broadcasted_iota(jnp.int32, shape, dim)


def total(x):
    return jnp.sum(jnp.sum(x, axis=0, keepdims=True), axis=1, keepdims=True)


def stream(src, dst, sems, sizes):
    copies = {}
    at = 0
    for c, size in enumerate(sizes):
        copies[at] = pltpu.make_async_copy(src.at[pl.ds(at, size)], dst.at[pl.ds(at, size)], sems.at[c])
        at += size
    return copies


def start_order(blocks, jac):
    order = list(blocks.values())
    for one in order[:AHEAD]:
        one.start()
    then = {at: [] for at in blocks}
    for at, one in zip(blocks, order[AHEAD:]):
        then[at].append(one)
    if START_JAC < 0:
        for one in jac.values():
            one.start()
    else:
        then[START_JAC] += list(jac.values())
    return then


def block_solve(x, blocks, copies, then):
    row = iota((16, BLOCK), 0) % 8
    parts = []
    for g in range(E // 8):
        hi, lo = split(x[8 * g : 8 * g + 8])
        both = jnp.concatenate([hi, lo], axis=0)
        acc = None
        for k in range(8):
            e = 8 * g + k
            if e in copies:
                copies[e].wait()
                for later in then.get(e, ()):
                    later.start()
            one = dot(jnp.where(row == k, both, 0.0).astype(BF16), blocks[e])
            acc = one if acc is None else acc + one
        parts.append(acc[:8] + acc[8:])
    return jnp.concatenate(parts, axis=0)


def point_masks(recv_node, counts):
    elem = lax.shift_right_logical(recv_node, 6)
    node = jnp.bitwise_and(recv_node, NODES - 1)
    node_hot = (iota((NODES, RPTS), 0) == node).astype(F32).astype(BF16)
    lane = iota((1, RPTS), 1)
    block = lax.shift_right_logical(lane, 7)
    count = jnp.where(
        block == 0, counts[0], jnp.where(block == 1, counts[1], jnp.where(block == 2, counts[2], counts[3]))
    )
    live = jnp.bitwise_and(lane, 127) < count
    elem_hot = (iota((E, RPTS), 0) == jnp.where(live, elem, -1)).astype(F32)
    return node_hot, elem_hot


def pick(z, masks):
    node_hot, elem_hot = masks
    hi, lo = split(z)
    rows = [part[:, v * NODES : (v + 1) * NODES] for part in (hi, lo) for v in range(VARS)]
    rows = jnp.concatenate(rows, axis=0).astype(BF16)
    at_node = dot(rows, node_hot)
    at_node = at_node[: VARS * E] + at_node[VARS * E :]
    return [
        jnp.sum(at_node[v * E : (v + 1) * E] * elem_hot, axis=0, keepdims=True)
        for v in range(VARS)
    ]


def pack(owner_hot, rank, comps):
    slot = iota((CAP, RPTS), 0) == rank
    rows = [jnp.where(slot, comp, 0.0) for comp in comps]
    rows.append(jnp.zeros((PEERS - CAP * len(comps), RPTS), F32))
    rows = jnp.concatenate(rows, axis=0)
    hi, rest = split(rows)
    mid, low = split(rest)
    out = dot_nt(owner_hot, jnp.concatenate([hi, mid, low], axis=0).astype(BF16))
    return (out[:, :PEERS] + out[:, PEERS : 2 * PEERS]) + out[:, 2 * PEERS :]


def owner_one_hot(owners):
    return (iota((PEERS, RPTS), 0) == owners).astype(F32)


def lagrange(coord):
    factors = []
    for k in range(4):
        factor = None
        for m in range(4):
            if m != k:
                one = (coord - GLL[m]) * (1.0 / (GLL[k] - GLL[m]))
                factor = one if factor is None else factor * one
        factors.append(factor)
    return factors


def interpolate(values, geometry, table):
    values = values.T
    geometry = geometry.T
    val = [values[8 * c : 8 * c + 8] for c in range(VARS)]
    parts = [split(one) for one in val]
    coords = [geometry[8 * (VARS + c) : 8 * (VARS + c) + 8] for c in range(3)]
    rows = [one for coord in coords for one in lagrange(coord)]
    rows.append(geometry[8 * (VARS + 3) : 8 * (VARS + 3) + 8])
    rows += [part[0] for part in parts] + [part[1] for part in parts]
    for c, one in enumerate(rows):
        table[8 * c : 8 * c + 8, :] = one
    sub = iota((8, PEERS), 0)
    elem_id = iota((E, PEERS), 0).astype(F32)
    left = []
    right = []
    for k in range(CAP):

        def row(c):
            return table[pl.ds(8 * c + k, 1), :]

        inner = sub % 4
        along_z = jnp.where(
            inner == 0, row(8), jnp.where(inner == 1, row(9), jnp.where(inner == 2, row(10), row(11)))
        )
        lower = jnp.where(sub < 4, row(4), row(5)) * along_z
        upper = jnp.where(sub < 4, row(6), row(7)) * along_z
        basis = jnp.concatenate(
            [half * row(i) for i in range(4) for half in (lower, upper)], axis=0
        )
        hi, lo = split(basis)
        right.append(jnp.concatenate([hi, lo], axis=0).astype(BF16))
        mask = elem_id == row(12)
        left.append(
            jnp.concatenate(
                [jnp.where(mask, row(13 + c), 0.0) for c in range(2 * VARS)], axis=0
            ).astype(BF16)
        )
    out = dot_nt(jnp.concatenate(left, axis=1), jnp.concatenate(right, axis=1))
    half = VARS * E
    out = out[:half, :NODES] + (out[:half, NODES:] + out[half:, :NODES])
    return jnp.concatenate([out[v * E : (v + 1) * E] for v in range(VARS)], axis=1)


def face_traces(z, jac, copies, spread, traces, outs):
    hi, lo = split(z)
    traces[...] = dot_nt(jnp.concatenate([hi, lo], axis=0).astype(BF16), spread)
    own_face = iota((16, 6 * FACEW), 1) // FACEW == iota((16, 6 * FACEW), 0) % 8
    for e in range(E):
        if e in copies:
            copies[e].wait()
        both = jnp.concatenate(
            [
                jnp.broadcast_to(traces[pl.ds(e, 1), :], (8, 6 * FACEW)),
                jnp.broadcast_to(traces[pl.ds(E + e, 1), :], (8, 6 * FACEW)),
            ],
            axis=0,
        )
        one = dot(jnp.where(own_face, both, 0.0).astype(BF16), jac[e])
        outs[8 * e : 8 * e + 8, 0:FACEW] = one[:8] + one[8:]
    return jnp.concatenate(
        [outs[pl.ds(f, E, stride=8), :][:, :FACEW] for f in range(6)], axis=0
    )


def faces(x, z, jac, copies, hots, spread_ref, base_ref, first_ref, second_ref, traces, outs):
    out = face_traces(z, jac, copies, spread_ref[...], traces, outs)
    hi, lo = split(out)
    hi, lo = hi.astype(BF16), lo.astype(BF16)
    local_hot, iface_hot = hots
    outgoing = dot(iface_hot, hi) + dot(iface_hot, lo)
    odd = lax.axis_index("dom") % 2 == 1
    low, high = outgoing[:E], outgoing[E:]
    first_ref[...] = jnp.where(odd, low, high)
    second_ref[...] = jnp.where(odd, high, low)
    base_ref[...] = x - spread_faces(dot_tn(local_hot, hi), dot_tn(local_hot, lo), spread_ref)


def first_kernel(
    x_hbm, blocks_hbm, jac_hbm, node_hbm, owner_hbm, elem_hbm, coord_hbm, count_hbm, nbr_hbm, spread_hbm,
    base_ref, first_ref, second_ref, pay_ref, rank_ref,
    x_ref, node_ref, owner_ref, elem_ref, coord_ref, count_ref, nbr_ref, spread_ref, small_sems,
    blocks, block_sems, jac, jac_sems, traces, outs,
):
    small = [
        pltpu.make_async_copy(src, dst, small_sems.at[i])
        for i, (src, dst) in enumerate(
            [
                (owner_hbm, owner_ref), (x_hbm, x_ref), (node_hbm, node_ref), (elem_hbm, elem_ref),
                (coord_hbm, coord_ref), (count_hbm, count_ref), (nbr_hbm, nbr_ref), (spread_hbm, spread_ref),
            ]
        )
    ]
    block_copies = stream(blocks_hbm, blocks, block_sems, BLOCK_CHUNKS)
    jac_copies = stream(jac_hbm, jac, jac_sems, JAC_CHUNKS)
    for one in small[:2]:
        one.start()
    then = start_order(block_copies, jac_copies)
    for one in small[2:]:
        one.start()
    for one in small[:2]:
        one.wait()
    hot = owner_one_hot(owner_ref[...])
    hot16 = hot.astype(BF16)
    earlier = (iota((RPTS, RPTS), 0) < iota((RPTS, RPTS), 1)).astype(F32).astype(BF16)
    rank = jnp.sum(hot * dot(hot16, earlier), axis=0, keepdims=True).astype(jnp.int32)
    rank_ref[...] = rank
    x = x_ref[...]
    z = block_solve(x, blocks, block_copies, then)
    for one in small[2:]:
        one.wait()
    masks = point_masks(node_ref[...], [count_ref[0, i] for i in range(4)])
    comps = pick(z, masks)
    comps += [coord_ref[c : c + 1, :] for c in range(3)]
    comps.append(elem_ref[...].astype(F32))
    pay_ref[...] = pack(hot16, rank, comps)
    faces(x, z, jac, jac_copies, neighbour_one_hots(nbr_ref[...]), spread_ref, base_ref, first_ref, second_ref, traces, outs)


def neighbour_one_hots(nbr):
    target = jnp.concatenate(
        [
            jnp.where(nbr[f : f + 1] < 0, -1, jnp.where(nbr[f : f + 1] < E, nbr[f : f + 1] + (f ^ 1) * E, nbr[f : f + 1] + 5 * E))
            for f in range(6)
        ],
        axis=1,
    )
    hot = (iota((8 * E, 6 * E), 0) == target).astype(F32).astype(BF16)
    return hot[: 6 * E], hot[6 * E :]


def spread_faces(hi, lo, spread_ref):
    acc = None
    for f in range(6):
        both = jnp.concatenate([hi[f * E : (f + 1) * E], lo[f * E : (f + 1) * E]], axis=0)
        one = dot(both.astype(BF16), spread_ref[f * FACEW : (f + 1) * FACEW, :])
        acc = one if acc is None else acc + one
    return acc[:E] + acc[E:]


def arrived_kernel(base_ref, first_ref, second_ref, nbr_ref, spread_ref, out_ref):
    odd = lax.axis_index("dom") % 2 == 1
    first, second = first_ref[...], second_ref[...]
    low, high = jnp.where(odd, first, second), jnp.where(odd, second, first)
    hi, lo = split(jnp.concatenate([low, high], axis=0))
    _, iface_hot = neighbour_one_hots(nbr_ref[...])
    hi, lo = dot_tn(iface_hot, hi.astype(BF16)), dot_tn(iface_hot, lo.astype(BF16))
    out_ref[...] = base_ref[...] - spread_faces(hi, lo, spread_ref)


def with_scalars(table, scalars):
    lane = iota(table.shape, 1)
    for i, one in enumerate(scalars):
        table = jnp.where(lane == SCALAR_LANE + i, one, table)
    return table


def read_scalars(table, count):
    row = jnp.sum(table, axis=0, keepdims=True)
    return [row[:, SCALAR_LANE + i : SCALAR_LANE + i + 1] for i in range(count)]


def second_kernel(
    base_ref, got_ref, b_ref, blocks_hbm, jac_hbm, node_ref, owner_ref, rank_ref, count_ref, nbr_ref, spread_ref,
    u_ref, out_ref, first_ref, second_ref, pay_ref,
    table, blocks, block_sems, jac, jac_sems, traces, outs,
):
    block_copies = stream(blocks_hbm, blocks, block_sems, BLOCK_CHUNKS)
    jac_copies = stream(jac_hbm, jac, jac_sems, JAC_CHUNKS)
    then = start_order(block_copies, jac_copies)
    got = got_ref[...]
    u = base_ref[...] - interpolate(got, got, table)
    u_ref[...] = u
    b = b_ref[...]
    scalars = [total(b * b), total(b * u)]
    z = block_solve(u, blocks, block_copies, then)
    masks = point_masks(node_ref[...], [count_ref[0, i] for i in range(4)])
    hot = owner_one_hot(owner_ref[...]).astype(BF16)
    pay_ref[...] = with_scalars(pack(hot, rank_ref[...], pick(z, masks)), scalars)
    faces(u, z, jac, jac_copies, neighbour_one_hots(nbr_ref[...]), spread_ref, out_ref, first_ref, second_ref, traces, outs)


def third_kernel(base_ref, got_ref, first_ref, b_ref, u_ref, rest_ref, pay_ref, known_ref, table):
    got = got_ref[...]
    w = base_ref[...] - interpolate(got, first_ref[...], table)
    bb, bu = read_scalars(got, 2)
    h00 = bu / (bb + EPS)
    b = b_ref[...]
    u = u_ref[...]
    rest = u - h00 * b
    mapped = w - h00 * u
    rest_ref[...] = rest
    scalars = [
        total(rest * rest), total(b * rest), total(mapped * b), total(mapped * rest), total(mapped * mapped),
    ]
    pay_ref[...] = with_scalars(jnp.zeros((PEERS, PEERS), F32), scalars)
    known_ref[...] = with_scalars(jnp.zeros((8, PEERS), F32), [bb * 0.125, bu * 0.125])


def last_kernel(got_ref, known_ref, b_ref, rest_ref, out_ref):
    bb, bu = read_scalars(known_ref[...], 2)
    rr, br, mb, mr, mm = read_scalars(got_ref[...], 5)
    s2 = bb + EPS
    start = jnp.sqrt(s2)
    h00 = bu / s2
    h10 = jnp.sqrt(rr / s2 + EPS)
    h01 = mb / (s2 * h10)
    scale = s2 * (h10 * h10)
    h11 = mr / scale
    left = (
        mm / scale
        - h01 * h01 * (2.0 - bb / s2)
        - h11 * h11 * (2.0 - rr / scale)
        + 2.0 * h01 * h11 * (br / (s2 * h10))
    )
    h21 = jnp.sqrt(jnp.maximum(left, 0.0) + EPS)
    r00 = jnp.sqrt(h00 * h00 + h10 * h10)
    c0 = h00 / r00
    s0 = h10 / r00
    r01 = c0 * h01 + s0 * h11
    low = c0 * h11 - s0 * h01
    r11 = jnp.sqrt(low * low + h21 * h21)
    c1 = low / r11
    y1 = c1 * (-s0 * start) / r11
    y0 = (c0 * start - r01 * y1) / r00
    out_ref[...] = (y0 / start) * b_ref[...] + (y1 / (start * h10)) * rest_ref[...]


VM = pl.BlockSpec(memory_space=pltpu.VMEM)
SM = pl.BlockSpec(memory_space=pltpu.SMEM)


HBM = pl.BlockSpec(memory_space=pltpu.HBM)


def swaps(start, ends):
    return [pair for i in range(start, ends, 2) for pair in ((i, i + 1), (i + 1, i))]


def in_hbm(x):
    return pltpu.with_memory_space_constraint(x, pltpu.HBM)


def call(kernel, in_specs, outs, scratch, *args):
    return pl.pallas_call(
        kernel,
        in_specs=in_specs,
        out_specs=[VM] * len(outs),
        out_shape=[jax.ShapeDtypeStruct(shape, dtype) for shape, dtype in outs],
        scratch_shapes=scratch,
        compiler_params=pltpu.CompilerParams(vmem_limit_bytes=VMEM_LIMIT),
        name=kernel.__name__,
    )(*args)


def exchange(table):
    return lax.all_to_all(
        table.reshape(PEERS, 1, PEERS), AXES, split_axis=0, concat_axis=0, tiled=True
    ).reshape(PEERS, PEERS)


def local(
    grad_rhs, block_inv, face_jac, face_nbr, recv_node, owners, donor_elem, donor_coords, recv_counts
):
    jac = face_jac.reshape(E, 6 * FACEW, FACEW)
    nbr = face_nbr.T
    node = recv_node.reshape(1, RPTS)
    owner = owners.reshape(1, RPTS)
    elem = donor_elem.reshape(1, RPTS)
    spread = jnp.asarray(spread_matrix(), BF16)
    ends = lax.axis_size("dom") - 1
    even_pairs = swaps(0, ends)
    odd_pairs = swaps(1, ends)
    full = ((E, BLOCK), F32)
    table = ((PEERS, PEERS), F32)
    half = ((E, FACEW), F32)
    row = pltpu.VMEM((1, RPTS), jnp.int32)
    matrices = [
        pltpu.VMEM((E, BLOCK, BLOCK), BF16), pltpu.SemaphoreType.DMA((len(BLOCK_CHUNKS),)),
        pltpu.VMEM((E, 6 * FACEW, FACEW), BF16), pltpu.SemaphoreType.DMA((len(JAC_CHUNKS),)),
    ]
    face_scratch = [pltpu.VMEM((2 * E, 6 * FACEW), F32), pltpu.VMEM((8 * E, PEERS), F32)]
    rows_scratch = pltpu.VMEM((8 * (13 + 2 * VARS), PEERS), F32)

    def arrive(base, first, second):
        second = lax.ppermute(second, "dom", odd_pairs)
        first = lax.ppermute(first, "dom", even_pairs)
        return call(arrived_kernel, [VM] * 5, [full], [], base, first, second, nbr, spread)[0]

    small = (node, owner, elem, donor_coords, recv_counts, nbr, spread)
    base, first, second, pay, rank = call(
        first_kernel,
        [HBM] * 10,
        [full, half, half, table, ((1, RPTS), jnp.int32)],
        [
            pltpu.VMEM((E, BLOCK), F32), row, row, row, pltpu.VMEM((3, RPTS), F32),
            pltpu.SMEM((1, 4), jnp.int32), pltpu.VMEM((6, E), jnp.int32),
            pltpu.VMEM((6 * FACEW, BLOCK), BF16), pltpu.SemaphoreType.DMA((8,)),
        ]
        + matrices
        + face_scratch,
        *[in_hbm(one) for one in (grad_rhs, block_inv, jac) + small],
    )
    got1 = exchange(pay)
    base = arrive(base, first, second)
    u, base, first, second, pay = call(
        second_kernel,
        [VM] * 3 + [HBM] * 2 + [VM] * 3 + [SM, VM, VM],
        [full, full, half, half, table],
        [rows_scratch] + matrices + face_scratch,
        base, got1, grad_rhs, in_hbm(block_inv), in_hbm(jac), node, owner, rank, recv_counts, nbr, spread,
    )
    got2 = exchange(pay)
    base = arrive(base, first, second)
    rest, pay, known = call(
        third_kernel,
        [VM] * 5,
        [full, table, ((8, PEERS), F32)],
        [rows_scratch],
        base, got2, got1, grad_rhs, u,
    )
    got3 = exchange(pay)
    return call(last_kernel, [VM] * 4, [full], [], got3, known, grad_rhs, rest)[0]


def solution(mesh):
    placed = (
        P(AXES, None),
        P(AXES, None, None),
        P(AXES, None, None, None),
        P(AXES, None),
        P(AXES),
        P(AXES, None),
        P(AXES),
        P(None, AXES),
        P(AXES, None),
    )
    return jax.shard_map(
        local, mesh=mesh, in_specs=placed, out_specs=P(AXES, None), check_vma=False
    )
```

```python
import jax
import jax.numpy as jnp
import numpy as np
from jax import lax
from jax.experimental import pallas as pl
from jax.experimental.pallas import tpu as pltpu
from jax.sharding import PartitionSpec as P

AXES = ("grp", "dom")
VARS = 5
NODES = 64
BLOCK = 320
FACEW = 80
E = 32
PEERS = 128
CAP = 8
RPTS = 512
BLOCK_CHUNKS = (16, 16)
START_JAC = 0
AHEAD = 2
JAC_CHUNKS = (16, 16)
SCALAR_LANE = 96
GLL = (-1.0, -0.4472135954999579, 0.4472135954999579, 1.0)
EPS = 1e-06
F32 = jnp.float32
BF16 = jnp.bfloat16
VMEM_LIMIT = 24 * 1024 * 1024


def face_table():
    grid = np.arange(64).reshape(4, 4, 4)
    faces = [grid[0], grid[3], grid[:, 0], grid[:, 3], grid[:, :, 0], grid[:, :, 3]]
    return np.stack([one.reshape(16) for one in faces])


def spread_matrix():
    table = face_table()
    out = np.zeros((6, VARS, 16, BLOCK), np.float32)
    for f in range(6):
        for v in range(VARS):
            out[f, v, np.arange(16), v * NODES + table[f]] = 1.0
    return out.reshape(6 * FACEW, BLOCK)


def dot(a, b):
    return jnp.dot(a, b, preferred_element_type=F32)


def dot_nt(a, b):
    return lax.dot_general(a, b, (((1,), (1,)), ((), ())), preferred_element_type=F32)


def dot_tn(a, b):
    return lax.dot_general(a, b, (((0,), (0,)), ((), ())), preferred_element_type=F32)


def split(x):
    hi = x.astype(BF16).astype(F32)
    return hi, x - hi


def iota(shape, dim):
    return lax.broadcasted_iota(jnp.int32, shape, dim)


def total(x):
    return jnp.sum(jnp.sum(x, axis=0, keepdims=True), axis=1, keepdims=True)


def stream(src, dst, sems, sizes):
    copies = {}
    at = 0
    for c, size in enumerate(sizes):
        copies[at] = pltpu.make_async_copy(src.at[pl.ds(at, size)], dst.at[pl.ds(at, size)], sems.at[c])
        at += size
    return copies


def start_order(blocks, jac):
    order = list(blocks.values())
    for one in order[:AHEAD]:
        one.start()
    then = {at: [] for at in blocks}
    for at, one in zip(blocks, order[AHEAD:]):
        then[at].append(one)
    if START_JAC < 0:
        for one in jac.values():
            one.start()
    else:
        then[START_JAC] += list(jac.values())
    return then


def block_solve(x, blocks, copies, then):
    row = iota((16, BLOCK), 0) % 8
    parts = []
    for g in range(E // 8):
        hi, lo = split(x[8 * g : 8 * g + 8])
        both = jnp.concatenate([hi, lo], axis=0)
        acc = None
        for k in range(8):
            e = 8 * g + k
            if e in copies:
                copies[e].wait()
                for later in then.get(e, ()):
                    later.start()
            one = dot(jnp.where(row == k, both, 0.0).astype(BF16), blocks[e])
            acc = one if acc is None else acc + one
        parts.append(acc[:8] + acc[8:])
    return jnp.concatenate(parts, axis=0)


def point_masks(recv_node, counts):
    elem = lax.shift_right_logical(recv_node, 6)
    node = jnp.bitwise_and(recv_node, NODES - 1)
    node_hot = (iota((NODES, RPTS), 0) == node).astype(F32).astype(BF16)
    lane = iota((1, RPTS), 1)
    block = lax.shift_right_logical(lane, 7)
    count = jnp.where(
        block == 0, counts[0], jnp.where(block == 1, counts[1], jnp.where(block == 2, counts[2], counts[3]))
    )
    live = jnp.bitwise_and(lane, 127) < count
    elem_hot = (iota((E, RPTS), 0) == jnp.where(live, elem, -1)).astype(F32)
    return node_hot, elem_hot


def pick(z, masks):
    node_hot, elem_hot = masks
    hi, lo = split(z)
    rows = [part[:, v * NODES : (v + 1) * NODES] for part in (hi, lo) for v in range(VARS)]
    rows = jnp.concatenate(rows, axis=0).astype(BF16)
    at_node = dot(rows, node_hot)
    at_node = at_node[: VARS * E] + at_node[VARS * E :]
    return [
        jnp.sum(at_node[v * E : (v + 1) * E] * elem_hot, axis=0, keepdims=True)
        for v in range(VARS)
    ]


def pack(owner_hot, rank, comps):
    slot = iota((CAP, RPTS), 0) == rank
    rows = [jnp.where(slot, comp, 0.0) for comp in comps]
    rows.append(jnp.zeros((PEERS - CAP * len(comps), RPTS), F32))
    rows = jnp.concatenate(rows, axis=0)
    hi, rest = split(rows)
    mid, low = split(rest)
    out = dot_nt(owner_hot, jnp.concatenate([hi, mid, low], axis=0).astype(BF16))
    return (out[:, :PEERS] + out[:, PEERS : 2 * PEERS]) + out[:, 2 * PEERS :]


def owner_one_hot(owners):
    return (iota((PEERS, RPTS), 0) == owners).astype(F32)


def lagrange(coord):
    factors = []
    for k in range(4):
        factor = None
        for m in range(4):
            if m != k:
                one = (coord - GLL[m]) * (1.0 / (GLL[k] - GLL[m]))
                factor = one if factor is None else factor * one
        factors.append(factor)
    return factors


def interpolate(values, geometry, table):
    values = values.T
    geometry = geometry.T
    val = [values[8 * c : 8 * c + 8] for c in range(VARS)]
    parts = [split(one) for one in val]
    coords = [geometry[8 * (VARS + c) : 8 * (VARS + c) + 8] for c in range(3)]
    rows = [one for coord in coords for one in lagrange(coord)]
    rows.append(geometry[8 * (VARS + 3) : 8 * (VARS + 3) + 8])
    rows += [part[0] for part in parts] + [part[1] for part in parts]
    for c, one in enumerate(rows):
        table[8 * c : 8 * c + 8, :] = one
    sub = iota((8, PEERS), 0)
    elem_id = iota((E, PEERS), 0).astype(F32)
    left = []
    right = []
    for k in range(CAP):

        def row(c):
            return table[pl.ds(8 * c + k, 1), :]

        inner = sub % 4
        along_z = jnp.where(
            inner == 0, row(8), jnp.where(inner == 1, row(9), jnp.where(inner == 2, row(10), row(11)))
        )
        lower = jnp.where(sub < 4, row(4), row(5)) * along_z
        upper = jnp.where(sub < 4, row(6), row(7)) * along_z
        basis = jnp.concatenate(
            [half * row(i) for i in range(4) for half in (lower, upper)], axis=0
        )
        hi, lo = split(basis)
        right.append(jnp.concatenate([hi, lo], axis=0).astype(BF16))
        mask = elem_id == row(12)
        left.append(
            jnp.concatenate(
                [jnp.where(mask, row(13 + c), 0.0) for c in range(2 * VARS)], axis=0
            ).astype(BF16)
        )
    out = dot_nt(jnp.concatenate(left, axis=1), jnp.concatenate(right, axis=1))
    half = VARS * E
    out = out[:half, :NODES] + (out[:half, NODES:] + out[half:, :NODES])
    return jnp.concatenate([out[v * E : (v + 1) * E] for v in range(VARS)], axis=1)


def face_traces(z, jac, copies, spread, traces, outs):
    hi, lo = split(z)
    traces[...] = dot_nt(jnp.concatenate([hi, lo], axis=0).astype(BF16), spread)
    own_face = iota((16, 6 * FACEW), 1) // FACEW == iota((16, 6 * FACEW), 0) % 8
    for e in range(E):
        if e in copies:
            copies[e].wait()
        both = jnp.concatenate(
            [
                jnp.broadcast_to(traces[pl.ds(e, 1), :], (8, 6 * FACEW)),
                jnp.broadcast_to(traces[pl.ds(E + e, 1), :], (8, 6 * FACEW)),
            ],
            axis=0,
        )
        one = dot(jnp.where(own_face, both, 0.0).astype(BF16), jac[e])
        outs[8 * e : 8 * e + 8, 0:FACEW] = one[:8] + one[8:]
    return jnp.concatenate(
        [outs[pl.ds(f, E, stride=8), :][:, :FACEW] for f in range(6)], axis=0
    )


def faces(x, z, jac, copies, hots, spread_ref, base_ref, first_ref, second_ref, traces, outs):
    out = face_traces(z, jac, copies, spread_ref[...], traces, outs)
    hi, lo = split(out)
    hi, lo = hi.astype(BF16), lo.astype(BF16)
    local_hot, iface_hot = hots
    outgoing = dot(iface_hot, hi) + dot(iface_hot, lo)
    odd = lax.axis_index("dom") % 2 == 1
    low, high = outgoing[:E], outgoing[E:]
    first_ref[...] = jnp.where(odd, low, high)
    second_ref[...] = jnp.where(odd, high, low)
    base_ref[...] = x - spread_faces(dot_tn(local_hot, hi), dot_tn(local_hot, lo), spread_ref)


def first_kernel(
    x_hbm, blocks_hbm, jac_hbm, node_hbm, owner_hbm, elem_hbm, coord_hbm, count_hbm, nbr_hbm, spread_hbm,
    base_ref, first_ref, second_ref, pay_ref, rank_ref,
    x_ref, node_ref, owner_ref, elem_ref, coord_ref, count_ref, nbr_ref, spread_ref, small_sems,
    blocks, block_sems, jac, jac_sems, traces, outs,
):
    small = [
        pltpu.make_async_copy(src, dst, small_sems.at[i])
        for i, (src, dst) in enumerate(
            [
                (owner_hbm, owner_ref), (x_hbm, x_ref), (node_hbm, node_ref), (elem_hbm, elem_ref),
                (coord_hbm, coord_ref), (count_hbm, count_ref), (nbr_hbm, nbr_ref), (spread_hbm, spread_ref),
            ]
        )
    ]
    block_copies = stream(blocks_hbm, blocks, block_sems, BLOCK_CHUNKS)
    jac_copies = stream(jac_hbm, jac, jac_sems, JAC_CHUNKS)
    for one in small[:2]:
        one.start()
    then = start_order(block_copies, jac_copies)
    for one in small[2:]:
        one.start()
    for one in small[:2]:
        one.wait()
    hot = owner_one_hot(owner_ref[...])
    hot16 = hot.astype(BF16)
    earlier = (iota((RPTS, RPTS), 0) < iota((RPTS, RPTS), 1)).astype(F32).astype(BF16)
    rank = jnp.sum(hot * dot(hot16, earlier), axis=0, keepdims=True).astype(jnp.int32)
    rank_ref[...] = rank
    x = x_ref[...]
    z = block_solve(x, blocks, block_copies, then)
    for one in small[2:]:
        one.wait()
    masks = point_masks(node_ref[...], [count_ref[0, i] for i in range(4)])
    comps = pick(z, masks)
    comps += [coord_ref[c : c + 1, :] for c in range(3)]
    comps.append(elem_ref[...].astype(F32))
    pay_ref[...] = pack(hot16, rank, comps)
    faces(x, z, jac, jac_copies, neighbour_one_hots(nbr_ref[...]), spread_ref, base_ref, first_ref, second_ref, traces, outs)


def neighbour_one_hots(nbr):
    target = jnp.concatenate(
        [
            jnp.where(nbr[f : f + 1] < 0, -1, jnp.where(nbr[f : f + 1] < E, nbr[f : f + 1] + (f ^ 1) * E, nbr[f : f + 1] + 5 * E))
            for f in range(6)
        ],
        axis=1,
    )
    hot = (iota((8 * E, 6 * E), 0) == target).astype(F32).astype(BF16)
    return hot[: 6 * E], hot[6 * E :]


def spread_faces(hi, lo, spread_ref):
    acc = None
    for f in range(6):
        both = jnp.concatenate([hi[f * E : (f + 1) * E], lo[f * E : (f + 1) * E]], axis=0)
        one = dot(both.astype(BF16), spread_ref[f * FACEW : (f + 1) * FACEW, :])
        acc = one if acc is None else acc + one
    return acc[:E] + acc[E:]


def arrived(first, second, nbr, spread_ref):
    odd = lax.axis_index("dom") % 2 == 1
    low, high = jnp.where(odd, first, second), jnp.where(odd, second, first)
    hi, lo = split(jnp.concatenate([low, high], axis=0))
    _, iface_hot = neighbour_one_hots(nbr)
    hi, lo = dot_tn(iface_hot, hi.astype(BF16)), dot_tn(iface_hot, lo.astype(BF16))
    return spread_faces(hi, lo, spread_ref)


def late_interp_kernel(got_ref, first_ref, out_ref, table):
    out_ref[...] = interpolate(got_ref[...], first_ref[...], table)


def interp_kernel(got_ref, blocks_hbm, interp_ref, blocks_ref, table, sems):
    copies = list(stream(blocks_hbm, blocks_ref, sems, BLOCK_CHUNKS).values())
    for one in copies:
        one.start()
    got = got_ref[...]
    interp_ref[...] = interpolate(got, got, table)
    for one in copies:
        one.wait()


def with_scalars(table, scalars):
    lane = iota(table.shape, 1)
    for i, one in enumerate(scalars):
        table = jnp.where(lane == SCALAR_LANE + i, one, table)
    return table


def read_scalars(table, count):
    row = jnp.sum(table, axis=0, keepdims=True)
    return [row[:, SCALAR_LANE + i : SCALAR_LANE + i + 1] for i in range(count)]


def second_kernel(
    base_ref, first_in, second_in, interp_ref, b_ref, blocks_ref, jac_hbm,
    node_ref, owner_ref, rank_ref, count_ref, nbr_ref, spread_ref,
    u_ref, out_ref, first_ref, second_ref, pay_ref,
    jac, jac_sems, traces, outs,
):
    jac_copies = stream(jac_hbm, jac, jac_sems, JAC_CHUNKS)
    for one in jac_copies.values():
        one.start()
    b = b_ref[...]
    nbr = nbr_ref[...]
    u = base_ref[...] - interp_ref[...] - arrived(first_in[...], second_in[...], nbr, spread_ref)
    u_ref[...] = u
    scalars = [total(b * b), total(b * u)]
    z = block_solve(u, blocks_ref, {}, {})
    masks = point_masks(node_ref[...], [count_ref[0, i] for i in range(4)])
    hot = owner_one_hot(owner_ref[...]).astype(BF16)
    pay_ref[...] = with_scalars(pack(hot, rank_ref[...], pick(z, masks)), scalars)
    faces(u, z, jac, jac_copies, neighbour_one_hots(nbr), spread_ref, out_ref, first_ref, second_ref, traces, outs)


def third_kernel(
    base_ref, first_ref, second_ref, nbr_ref, spread_ref, interp_ref, got_ref, b_ref, u_ref,
    rest_ref, pay_ref, known_ref,
):
    late = arrived(first_ref[...], second_ref[...], nbr_ref[...], spread_ref)
    w = base_ref[...] - interp_ref[...] - late
    bb, bu = read_scalars(got_ref[...], 2)
    h00 = bu / (bb + EPS)
    b = b_ref[...]
    u = u_ref[...]
    rest = u - h00 * b
    mapped = w - h00 * u
    rest_ref[...] = rest
    scalars = [
        total(rest * rest), total(b * rest), total(mapped * b), total(mapped * rest), total(mapped * mapped),
    ]
    pay_ref[...] = with_scalars(jnp.zeros((PEERS, PEERS), F32), scalars)
    known_ref[...] = with_scalars(jnp.zeros((8, PEERS), F32), [bb * 0.125, bu * 0.125])


def last_kernel(got_ref, known_ref, b_ref, rest_ref, out_ref):
    bb, bu = read_scalars(known_ref[...], 2)
    rr, br, mb, mr, mm = read_scalars(got_ref[...], 5)
    s2 = bb + EPS
    start = jnp.sqrt(s2)
    h00 = bu / s2
    h10 = jnp.sqrt(rr / s2 + EPS)
    h01 = mb / (s2 * h10)
    scale = s2 * (h10 * h10)
    h11 = mr / scale
    left = (
        mm / scale
        - h01 * h01 * (2.0 - bb / s2)
        - h11 * h11 * (2.0 - rr / scale)
        + 2.0 * h01 * h11 * (br / (s2 * h10))
    )
    h21 = jnp.sqrt(jnp.maximum(left, 0.0) + EPS)
    r00 = jnp.sqrt(h00 * h00 + h10 * h10)
    c0 = h00 / r00
    s0 = h10 / r00
    r01 = c0 * h01 + s0 * h11
    low = c0 * h11 - s0 * h01
    r11 = jnp.sqrt(low * low + h21 * h21)
    c1 = low / r11
    y1 = c1 * (-s0 * start) / r11
    y0 = (c0 * start - r01 * y1) / r00
    out_ref[...] = (y0 / start) * b_ref[...] + (y1 / (start * h10)) * rest_ref[...]


VM = pl.BlockSpec(memory_space=pltpu.VMEM)
SM = pl.BlockSpec(memory_space=pltpu.SMEM)


HBM = pl.BlockSpec(memory_space=pltpu.HBM)


def swaps(start, ends):
    return [pair for i in range(start, ends, 2) for pair in ((i, i + 1), (i + 1, i))]


def in_hbm(x):
    return pltpu.with_memory_space_constraint(x, pltpu.HBM)


def call(kernel, in_specs, outs, scratch, *args):
    return pl.pallas_call(
        kernel,
        in_specs=in_specs,
        out_specs=[VM] * len(outs),
        out_shape=[jax.ShapeDtypeStruct(shape, dtype) for shape, dtype in outs],
        scratch_shapes=scratch,
        compiler_params=pltpu.CompilerParams(vmem_limit_bytes=VMEM_LIMIT),
        name=kernel.__name__,
    )(*args)


def exchange(table):
    return lax.all_to_all(
        table.reshape(PEERS, 1, PEERS), AXES, split_axis=0, concat_axis=0, tiled=True
    ).reshape(PEERS, PEERS)


def local(
    grad_rhs, block_inv, face_jac, face_nbr, recv_node, owners, donor_elem, donor_coords, recv_counts
):
    jac = face_jac.reshape(E, 6 * FACEW, FACEW)
    nbr = face_nbr.T
    node = recv_node.reshape(1, RPTS)
    owner = owners.reshape(1, RPTS)
    elem = donor_elem.reshape(1, RPTS)
    spread = jnp.asarray(spread_matrix(), BF16)
    ends = lax.axis_size("dom") - 1
    even_pairs = swaps(0, ends)
    odd_pairs = swaps(1, ends)
    full = ((E, BLOCK), F32)
    table = ((PEERS, PEERS), F32)
    half = ((E, FACEW), F32)
    row = pltpu.VMEM((1, RPTS), jnp.int32)
    matrices = [
        pltpu.VMEM((E, BLOCK, BLOCK), BF16), pltpu.SemaphoreType.DMA((len(BLOCK_CHUNKS),)),
        pltpu.VMEM((E, 6 * FACEW, FACEW), BF16), pltpu.SemaphoreType.DMA((len(JAC_CHUNKS),)),
    ]
    face_scratch = [pltpu.VMEM((2 * E, 6 * FACEW), F32), pltpu.VMEM((8 * E, PEERS), F32)]
    rows_scratch = pltpu.VMEM((8 * (13 + 2 * VARS), PEERS), F32)

    def swap(first, second):
        return lax.ppermute(first, "dom", even_pairs), lax.ppermute(second, "dom", odd_pairs)

    small = (node, owner, elem, donor_coords, recv_counts, nbr, spread)
    base, first, second, pay, rank = call(
        first_kernel,
        [HBM] * 10,
        [full, half, half, table, ((1, RPTS), jnp.int32)],
        [
            pltpu.VMEM((E, BLOCK), F32), row, row, row, pltpu.VMEM((3, RPTS), F32),
            pltpu.SMEM((1, 4), jnp.int32), pltpu.VMEM((6, E), jnp.int32),
            pltpu.VMEM((6 * FACEW, BLOCK), BF16), pltpu.SemaphoreType.DMA((8,)),
        ]
        + matrices
        + face_scratch,
        *[in_hbm(one) for one in (grad_rhs, block_inv, jac) + small],
    )
    got1 = exchange(pay)
    first, second = swap(first, second)
    interp, blocks = call(
        interp_kernel,
        [VM, HBM],
        [full, ((E, BLOCK, BLOCK), BF16)],
        [rows_scratch, matrices[1]],
        got1, in_hbm(block_inv),
    )
    u, base, first, second, pay = call(
        second_kernel,
        [VM] * 6 + [HBM] + [VM] * 3 + [SM, VM, VM],
        [full, full, half, half, table],
        matrices[2:] + face_scratch,
        base, first, second, interp, grad_rhs, blocks, in_hbm(jac), node, owner, rank, recv_counts, nbr, spread,
    )
    got2 = exchange(pay)
    first, second = swap(first, second)
    interp = call(late_interp_kernel, [VM, VM], [full], [rows_scratch], got2, got1)[0]
    rest, pay, known = call(
        third_kernel,
        [VM] * 9,
        [full, table, ((8, PEERS), F32)],
        [],
        base, first, second, nbr, spread, interp, got2, grad_rhs, u,
    )
    got3 = exchange(pay)
    return call(last_kernel, [VM] * 4, [full], [], got3, known, grad_rhs, rest)[0]


def solution(mesh):
    placed = (
        P(AXES, None),
        P(AXES, None, None),
        P(AXES, None, None, None),
        P(AXES, None),
        P(AXES),
        P(AXES, None),
        P(AXES),
        P(None, AXES),
        P(AXES, None),
    )
    return jax.shard_map(
        local, mesh=mesh, in_specs=placed, out_specs=P(AXES, None), check_vma=False
    )
```

```python
import jax
import jax.numpy as jnp
import numpy as np
from jax import lax
from jax.experimental import pallas as pl
from jax.experimental.pallas import tpu as pltpu
from jax.sharding import PartitionSpec as P

AXES = ("grp", "dom")
VARS = 5
NODES = 64
BLOCK = 320
FACEW = 80
E = 32
PEERS = 128
CAP = 8
RPTS = 512
BLOCK_CHUNKS = (8, 8, 16)
KEPT = 8
START_JAC = 0
AHEAD = 3
JAC_CHUNKS = (16, 16)
SCALAR_LANE = 96
GLL = (-1.0, -0.4472135954999579, 0.4472135954999579, 1.0)
EPS = 1e-06
F32 = jnp.float32
BF16 = jnp.bfloat16
VMEM_LIMIT = 24 * 1024 * 1024


def face_table():
    grid = np.arange(64).reshape(4, 4, 4)
    faces = [grid[0], grid[3], grid[:, 0], grid[:, 3], grid[:, :, 0], grid[:, :, 3]]
    return np.stack([one.reshape(16) for one in faces])


def spread_matrix():
    table = face_table()
    out = np.zeros((6, VARS, 16, BLOCK), np.float32)
    for f in range(6):
        for v in range(VARS):
            out[f, v, np.arange(16), v * NODES + table[f]] = 1.0
    return out.reshape(6 * FACEW, BLOCK)


def dot(a, b):
    return jnp.dot(a, b, preferred_element_type=F32)


def dot_nt(a, b):
    return lax.dot_general(a, b, (((1,), (1,)), ((), ())), preferred_element_type=F32)


def dot_tn(a, b):
    return lax.dot_general(a, b, (((0,), (0,)), ((), ())), preferred_element_type=F32)


def split(x):
    hi = x.astype(BF16).astype(F32)
    return hi, x - hi


def iota(shape, dim):
    return lax.broadcasted_iota(jnp.int32, shape, dim)


def total(x):
    return jnp.sum(jnp.sum(x, axis=0, keepdims=True), axis=1, keepdims=True)


def stream(src, dst, sems, sizes):
    copies = {}
    at = 0
    for c, size in enumerate(sizes):
        copies[at] = pltpu.make_async_copy(src.at[pl.ds(at, size)], dst.at[pl.ds(at, size)], sems.at[c])
        at += size
    return copies


def stream_blocks(src, kept, rest, sems):
    copies = {}
    at = 0
    for c, size in enumerate(BLOCK_CHUNKS):
        if at >= KEPT:
            copies[at] = pltpu.make_async_copy(
                src.at[pl.ds(at, size)], rest.at[pl.ds(at - KEPT, size)], sems.at[c]
            )
        elif kept is not None:
            copies[at] = pltpu.make_async_copy(src.at[pl.ds(at, size)], kept.at[pl.ds(at, size)], sems.at[c])
        at += size
    return copies


class Joined:
    def __init__(self, kept, rest):
        self.kept, self.rest = kept, rest

    def __getitem__(self, e):
        return self.kept[e] if e < KEPT else self.rest[e - KEPT]


def start_order(blocks, jac):
    order = list(blocks.values())
    for one in order[:AHEAD]:
        one.start()
    then = {at: [] for at in blocks}
    for at, one in zip(blocks, order[AHEAD:]):
        then[at].append(one)
    if START_JAC < 0:
        for one in jac.values():
            one.start()
    else:
        then[START_JAC] += list(jac.values())
    return then


def block_solve(x, blocks, copies, then):
    row = iota((16, BLOCK), 0) % 8
    parts = []
    for g in range(E // 8):
        hi, lo = split(x[8 * g : 8 * g + 8])
        both = jnp.concatenate([hi, lo], axis=0)
        acc = None
        for k in range(8):
            e = 8 * g + k
            if e in copies:
                copies[e].wait()
                for later in then.get(e, ()):
                    later.start()
            one = dot(jnp.where(row == k, both, 0.0).astype(BF16), blocks[e])
            acc = one if acc is None else acc + one
        parts.append(acc[:8] + acc[8:])
    return jnp.concatenate(parts, axis=0)


def point_masks(recv_node, counts):
    elem = lax.shift_right_logical(recv_node, 6)
    node = jnp.bitwise_and(recv_node, NODES - 1)
    node_hot = (iota((NODES, RPTS), 0) == node).astype(F32).astype(BF16)
    lane = iota((1, RPTS), 1)
    block = lax.shift_right_logical(lane, 7)
    count = jnp.where(
        block == 0, counts[0], jnp.where(block == 1, counts[1], jnp.where(block == 2, counts[2], counts[3]))
    )
    live = jnp.bitwise_and(lane, 127) < count
    elem_hot = (iota((E, RPTS), 0) == jnp.where(live, elem, -1)).astype(F32)
    return node_hot, elem_hot


def pick(z, masks):
    node_hot, elem_hot = masks
    hi, lo = split(z)
    rows = [part[:, v * NODES : (v + 1) * NODES] for part in (hi, lo) for v in range(VARS)]
    rows = jnp.concatenate(rows, axis=0).astype(BF16)
    at_node = dot(rows, node_hot)
    at_node = at_node[: VARS * E] + at_node[VARS * E :]
    return [
        jnp.sum(at_node[v * E : (v + 1) * E] * elem_hot, axis=0, keepdims=True)
        for v in range(VARS)
    ]


def pack(owner_hot, rank, comps):
    slot = iota((CAP, RPTS), 0) == rank
    rows = [jnp.where(slot, comp, 0.0) for comp in comps]
    rows.append(jnp.zeros((PEERS - CAP * len(comps), RPTS), F32))
    rows = jnp.concatenate(rows, axis=0)
    hi, rest = split(rows)
    mid, low = split(rest)
    out = dot_nt(owner_hot, jnp.concatenate([hi, mid, low], axis=0).astype(BF16))
    return (out[:, :PEERS] + out[:, PEERS : 2 * PEERS]) + out[:, 2 * PEERS :]


def owner_one_hot(owners):
    return (iota((PEERS, RPTS), 0) == owners).astype(F32)


def lagrange(coord):
    factors = []
    for k in range(4):
        factor = None
        for m in range(4):
            if m != k:
                one = (coord - GLL[m]) * (1.0 / (GLL[k] - GLL[m]))
                factor = one if factor is None else factor * one
        factors.append(factor)
    return factors


def interpolate(values, geometry, table):
    values = values.T
    geometry = geometry.T
    val = [values[8 * c : 8 * c + 8] for c in range(VARS)]
    parts = [split(one) for one in val]
    coords = [geometry[8 * (VARS + c) : 8 * (VARS + c) + 8] for c in range(3)]
    rows = [one for coord in coords for one in lagrange(coord)]
    rows.append(geometry[8 * (VARS + 3) : 8 * (VARS + 3) + 8])
    rows += [part[0] for part in parts] + [part[1] for part in parts]
    for c, one in enumerate(rows):
        table[8 * c : 8 * c + 8, :] = one
    sub = iota((8, PEERS), 0)
    elem_id = iota((E, PEERS), 0).astype(F32)
    left = []
    right = []
    for k in range(CAP):

        def row(c):
            return table[pl.ds(8 * c + k, 1), :]

        inner = sub % 4
        along_z = jnp.where(
            inner == 0, row(8), jnp.where(inner == 1, row(9), jnp.where(inner == 2, row(10), row(11)))
        )
        lower = jnp.where(sub < 4, row(4), row(5)) * along_z
        upper = jnp.where(sub < 4, row(6), row(7)) * along_z
        basis = jnp.concatenate(
            [half * row(i) for i in range(4) for half in (lower, upper)], axis=0
        )
        hi, lo = split(basis)
        right.append(jnp.concatenate([hi, lo], axis=0).astype(BF16))
        mask = elem_id == row(12)
        left.append(
            jnp.concatenate(
                [jnp.where(mask, row(13 + c), 0.0) for c in range(2 * VARS)], axis=0
            ).astype(BF16)
        )
    out = dot_nt(jnp.concatenate(left, axis=1), jnp.concatenate(right, axis=1))
    half = VARS * E
    out = out[:half, :NODES] + (out[:half, NODES:] + out[half:, :NODES])
    return jnp.concatenate([out[v * E : (v + 1) * E] for v in range(VARS)], axis=1)


def face_traces(z, jac, copies, spread, traces, outs):
    hi, lo = split(z)
    traces[...] = dot_nt(jnp.concatenate([hi, lo], axis=0).astype(BF16), spread)
    own_face = iota((16, 6 * FACEW), 1) // FACEW == iota((16, 6 * FACEW), 0) % 8
    for e in range(E):
        if e in copies:
            copies[e].wait()
        both = jnp.concatenate(
            [
                jnp.broadcast_to(traces[pl.ds(e, 1), :], (8, 6 * FACEW)),
                jnp.broadcast_to(traces[pl.ds(E + e, 1), :], (8, 6 * FACEW)),
            ],
            axis=0,
        )
        one = dot(jnp.where(own_face, both, 0.0).astype(BF16), jac[e])
        outs[8 * e : 8 * e + 8, 0:FACEW] = one[:8] + one[8:]
    return jnp.concatenate(
        [outs[pl.ds(f, E, stride=8), :][:, :FACEW] for f in range(6)], axis=0
    )


def faces(x, z, jac, copies, hots, spread_ref, base_ref, first_ref, second_ref, traces, outs):
    out = face_traces(z, jac, copies, spread_ref[...], traces, outs)
    hi, lo = split(out)
    hi, lo = hi.astype(BF16), lo.astype(BF16)
    local_hot, iface_hot = hots
    outgoing = dot(iface_hot, hi) + dot(iface_hot, lo)
    odd = lax.axis_index("dom") % 2 == 1
    low, high = outgoing[:E], outgoing[E:]
    first_ref[...] = jnp.where(odd, high, low)
    second_ref[...] = jnp.where(odd, low, high)
    base_ref[...] = x - spread_faces(dot_tn(local_hot, hi), dot_tn(local_hot, lo), spread_ref)


def first_kernel(
    x_hbm, blocks_hbm, jac_hbm, node_hbm, owner_hbm, elem_hbm, coord_hbm, count_hbm, nbr_hbm, spread_hbm,
    base_ref, first_ref, second_ref, pay_ref, rank_ref, kept_ref,
    x_ref, node_ref, owner_ref, elem_ref, coord_ref, count_ref, nbr_ref, spread_ref, small_sems,
    blocks, block_sems, jac, jac_sems, traces, outs,
):
    small = [
        pltpu.make_async_copy(src, dst, small_sems.at[i])
        for i, (src, dst) in enumerate(
            [
                (owner_hbm, owner_ref), (x_hbm, x_ref), (node_hbm, node_ref), (elem_hbm, elem_ref),
                (coord_hbm, coord_ref), (count_hbm, count_ref), (nbr_hbm, nbr_ref), (spread_hbm, spread_ref),
            ]
        )
    ]
    block_copies = stream_blocks(blocks_hbm, kept_ref, blocks, block_sems)
    jac_copies = stream(jac_hbm, jac, jac_sems, JAC_CHUNKS)
    for one in small[:2]:
        one.start()
    then = start_order(block_copies, jac_copies)
    for one in small[2:]:
        one.start()
    for one in small[:2]:
        one.wait()
    hot = owner_one_hot(owner_ref[...])
    hot16 = hot.astype(BF16)
    earlier = (iota((RPTS, RPTS), 0) < iota((RPTS, RPTS), 1)).astype(F32).astype(BF16)
    rank = jnp.sum(hot * dot(hot16, earlier), axis=0, keepdims=True).astype(jnp.int32)
    rank_ref[...] = rank
    x = x_ref[...]
    z = block_solve(x, Joined(kept_ref, blocks), block_copies, then)
    for one in small[2:]:
        one.wait()
    masks = point_masks(node_ref[...], [count_ref[0, i] for i in range(4)])
    comps = pick(z, masks)
    comps += [coord_ref[c : c + 1, :] for c in range(3)]
    comps.append(elem_ref[...].astype(F32))
    pay_ref[...] = pack(hot16, rank, comps)
    faces(x, z, jac, jac_copies, neighbour_one_hots(nbr_ref[...]), spread_ref, base_ref, first_ref, second_ref, traces, outs)


def neighbour_one_hots(nbr):
    target = jnp.concatenate(
        [
            jnp.where(nbr[f : f + 1] < 0, -1, jnp.where(nbr[f : f + 1] < E, nbr[f : f + 1] + (f ^ 1) * E, nbr[f : f + 1] + 5 * E))
            for f in range(6)
        ],
        axis=1,
    )
    hot = (iota((8 * E, 6 * E), 0) == target).astype(F32).astype(BF16)
    return hot[: 6 * E], hot[6 * E :]


def spread_faces(hi, lo, spread_ref):
    acc = None
    for f in range(6):
        both = jnp.concatenate([hi[f * E : (f + 1) * E], lo[f * E : (f + 1) * E]], axis=0)
        one = dot(both.astype(BF16), spread_ref[f * FACEW : (f + 1) * FACEW, :])
        acc = one if acc is None else acc + one
    return acc[:E] + acc[E:]


def arrived(first, second, nbr, spread_ref):
    odd = lax.axis_index("dom") % 2 == 1
    low, high = jnp.where(odd, second, first), jnp.where(odd, first, second)
    hi, lo = split(jnp.concatenate([low, high], axis=0))
    _, iface_hot = neighbour_one_hots(nbr)
    hi, lo = dot_tn(iface_hot, hi.astype(BF16)), dot_tn(iface_hot, lo.astype(BF16))
    return spread_faces(hi, lo, spread_ref)


def late_interp_kernel(got_ref, first_ref, out_ref, table):
    out_ref[...] = interpolate(got_ref[...], first_ref[...], table)


def interp_kernel(got_ref, blocks_hbm, interp_ref, blocks_ref, table, sems):
    copies = list(stream_blocks(blocks_hbm, None, blocks_ref, sems).values())
    for one in copies:
        one.start()
    got = got_ref[...]
    interp_ref[...] = interpolate(got, got, table)
    for one in copies:
        one.wait()


def with_scalars(table, scalars):
    lane = iota(table.shape, 1)
    for i, one in enumerate(scalars):
        table = jnp.where(lane == SCALAR_LANE + i, one, table)
    return table


def read_scalars(table, count):
    row = jnp.sum(table, axis=0, keepdims=True)
    return [row[:, SCALAR_LANE + i : SCALAR_LANE + i + 1] for i in range(count)]


def second_kernel(
    base_ref, first_in, second_in, interp_ref, b_ref, kept_ref, blocks_ref, jac_hbm,
    node_ref, owner_ref, rank_ref, count_ref, nbr_ref, spread_ref,
    u_ref, out_ref, first_ref, second_ref, pay_ref,
    jac, jac_sems, traces, outs,
):
    jac_copies = stream(jac_hbm, jac, jac_sems, (16, 16))
    for one in jac_copies.values():
        one.start()
    b = b_ref[...]
    nbr = nbr_ref[...]
    u = base_ref[...] - interp_ref[...] - arrived(first_in[...], second_in[...], nbr, spread_ref)
    u_ref[...] = u
    scalars = [total(b * b), total(b * u)]
    z = block_solve(u, Joined(kept_ref, blocks_ref), {}, {})
    jac_copies.pop(0).wait()
    masks = point_masks(node_ref[...], [count_ref[0, i] for i in range(4)])
    hot = owner_one_hot(owner_ref[...]).astype(BF16)
    pay_ref[...] = with_scalars(pack(hot, rank_ref[...], pick(z, masks)), scalars)
    jac_copies.pop(16).wait()
    faces(u, z, jac, jac_copies, neighbour_one_hots(nbr), spread_ref, out_ref, first_ref, second_ref, traces, outs)


def third_kernel(
    base_ref, first_ref, second_ref, nbr_ref, spread_ref, interp_ref, got_ref, b_ref, u_ref,
    rest_ref, pay_ref, known_ref,
):
    late = arrived(first_ref[...], second_ref[...], nbr_ref[...], spread_ref)
    w = base_ref[...] - interp_ref[...] - late
    bb, bu = read_scalars(got_ref[...], 2)
    h00 = bu / (bb + EPS)
    b = b_ref[...]
    u = u_ref[...]
    rest = u - h00 * b
    mapped = w - h00 * u
    rest_ref[...] = rest
    scalars = [
        total(rest * rest), total(b * rest), total(mapped * b), total(mapped * rest), total(mapped * mapped),
    ]
    pay_ref[...] = with_scalars(jnp.zeros((PEERS, PEERS), F32), scalars)
    known_ref[...] = with_scalars(jnp.zeros((8, PEERS), F32), [bb * 0.125, bu * 0.125])


def last_kernel(got_ref, known_ref, b_ref, rest_ref, out_ref):
    bb, bu = read_scalars(known_ref[...], 2)
    rr, br, mb, mr, mm = read_scalars(got_ref[...], 5)
    s2 = bb + EPS
    start = jnp.sqrt(s2)
    h00 = bu / s2
    h10 = jnp.sqrt(rr / s2 + EPS)
    h01 = mb / (s2 * h10)
    scale = s2 * (h10 * h10)
    h11 = mr / scale
    left = (
        mm / scale
        - h01 * h01 * (2.0 - bb / s2)
        - h11 * h11 * (2.0 - rr / scale)
        + 2.0 * h01 * h11 * (br / (s2 * h10))
    )
    h21 = jnp.sqrt(jnp.maximum(left, 0.0) + EPS)
    r00 = jnp.sqrt(h00 * h00 + h10 * h10)
    c0 = h00 / r00
    s0 = h10 / r00
    r01 = c0 * h01 + s0 * h11
    low = c0 * h11 - s0 * h01
    r11 = jnp.sqrt(low * low + h21 * h21)
    c1 = low / r11
    y1 = c1 * (-s0 * start) / r11
    y0 = (c0 * start - r01 * y1) / r00
    out_ref[...] = (y0 / start) * b_ref[...] + (y1 / (start * h10)) * rest_ref[...]


VM = pl.BlockSpec(memory_space=pltpu.VMEM)
SM = pl.BlockSpec(memory_space=pltpu.SMEM)


HBM = pl.BlockSpec(memory_space=pltpu.HBM)


def swaps(start, ends):
    return [pair for i in range(start, ends, 2) for pair in ((i, i + 1), (i + 1, i))]


def in_hbm(x):
    return pltpu.with_memory_space_constraint(x, pltpu.HBM)


def call(kernel, in_specs, outs, scratch, *args):
    return pl.pallas_call(
        kernel,
        in_specs=in_specs,
        out_specs=[VM] * len(outs),
        out_shape=[jax.ShapeDtypeStruct(shape, dtype) for shape, dtype in outs],
        scratch_shapes=scratch,
        compiler_params=pltpu.CompilerParams(vmem_limit_bytes=VMEM_LIMIT),
        name=kernel.__name__,
    )(*args)


def exchange(table):
    return lax.all_to_all(
        table.reshape(PEERS, 1, PEERS), AXES, split_axis=0, concat_axis=0, tiled=True
    ).reshape(PEERS, PEERS)


def local(
    grad_rhs, block_inv, face_jac, face_nbr, recv_node, owners, donor_elem, donor_coords, recv_counts
):
    jac = face_jac.reshape(E, 6 * FACEW, FACEW)
    nbr = face_nbr.T
    node = recv_node.reshape(1, RPTS)
    owner = owners.reshape(1, RPTS)
    elem = donor_elem.reshape(1, RPTS)
    spread = jnp.asarray(spread_matrix(), BF16)
    ends = lax.axis_size("dom") - 1
    even_pairs = swaps(0, ends)
    odd_pairs = swaps(1, ends)
    full = ((E, BLOCK), F32)
    table = ((PEERS, PEERS), F32)
    half = ((E, FACEW), F32)
    row = pltpu.VMEM((1, RPTS), jnp.int32)
    matrices = [
        pltpu.VMEM((E - KEPT, BLOCK, BLOCK), BF16), pltpu.SemaphoreType.DMA((len(BLOCK_CHUNKS),)),
        pltpu.VMEM((E, 6 * FACEW, FACEW), BF16), pltpu.SemaphoreType.DMA((2,)),
    ]
    face_scratch = [pltpu.VMEM((2 * E, 6 * FACEW), F32), pltpu.VMEM((8 * E, PEERS), F32)]
    rows_scratch = pltpu.VMEM((8 * (13 + 2 * VARS), PEERS), F32)

    def swap(first, second):
        return lax.ppermute(first, "dom", odd_pairs), lax.ppermute(second, "dom", even_pairs)

    small = (node, owner, elem, donor_coords, recv_counts, nbr, spread)
    base, first, second, pay, rank, kept = call(
        first_kernel,
        [HBM] * 10,
        [full, half, half, table, ((1, RPTS), jnp.int32), ((KEPT, BLOCK, BLOCK), BF16)],
        [
            pltpu.VMEM((E, BLOCK), F32), row, row, row, pltpu.VMEM((3, RPTS), F32),
            pltpu.SMEM((1, 4), jnp.int32), pltpu.VMEM((6, E), jnp.int32),
            pltpu.VMEM((6 * FACEW, BLOCK), BF16), pltpu.SemaphoreType.DMA((8,)),
        ]
        + matrices
        + face_scratch,
        *[in_hbm(one) for one in (grad_rhs, block_inv, jac) + small],
    )
    got1 = exchange(pay)
    first, second = swap(first, second)
    interp, blocks = call(
        interp_kernel,
        [VM, HBM],
        [full, ((E - KEPT, BLOCK, BLOCK), BF16)],
        [rows_scratch, matrices[1]],
        got1, in_hbm(block_inv),
    )
    u, base, first, second, pay = call(
        second_kernel,
        [VM] * 7 + [HBM] + [VM] * 3 + [SM, VM, VM],
        [full, full, half, half, table],
        matrices[2:] + face_scratch,
        base, first, second, interp, grad_rhs, kept, blocks, in_hbm(jac), node, owner, rank, recv_counts, nbr, spread,
    )
    got2 = exchange(pay)
    first, second = swap(first, second)
    interp = call(late_interp_kernel, [VM, VM], [full], [rows_scratch], got2, got1)[0]
    rest, pay, known = call(
        third_kernel,
        [VM] * 9,
        [full, table, ((8, PEERS), F32)],
        [],
        base, first, second, nbr, spread, interp, got2, grad_rhs, u,
    )
    got3 = exchange(pay)
    return call(last_kernel, [VM] * 4, [full], [], got3, known, grad_rhs, rest)[0]


def solution(mesh):
    placed = (
        P(AXES, None),
        P(AXES, None, None),
        P(AXES, None, None, None),
        P(AXES, None),
        P(AXES),
        P(AXES, None),
        P(AXES),
        P(None, AXES),
        P(AXES, None),
    )
    return jax.shard_map(
        local, mesh=mesh, in_specs=placed, out_specs=P(AXES, None), check_vma=False
    )
```

```python
import jax
import jax.numpy as jnp
import numpy as np
from jax import lax
from jax.experimental import pallas as pl
from jax.experimental.pallas import tpu as pltpu
from jax.sharding import PartitionSpec as P

AXES = ("grp", "dom")
VARS = 5
NODES = 64
BLOCK = 320
FACEW = 80
E = 32
PEERS = 128
CAP = 8
RPTS = 512
BLOCK_CHUNKS = (8, 8, 16)
KEPT = 8
START_JAC = 0
AHEAD = 3
JAC_CHUNKS = (16, 16)
SCALAR_LANE = 96
GLL = (-1.0, -0.4472135954999579, 0.4472135954999579, 1.0)
EPS = 1e-06
F32 = jnp.float32
BF16 = jnp.bfloat16
VMEM_LIMIT = 24 * 1024 * 1024


def face_table():
    grid = np.arange(64).reshape(4, 4, 4)
    faces = [grid[0], grid[3], grid[:, 0], grid[:, 3], grid[:, :, 0], grid[:, :, 3]]
    return np.stack([one.reshape(16) for one in faces])


def spread_matrix():
    table = face_table()
    out = np.zeros((6, VARS, 16, BLOCK), np.float32)
    for f in range(6):
        for v in range(VARS):
            out[f, v, np.arange(16), v * NODES + table[f]] = 1.0
    return out.reshape(6 * FACEW, BLOCK)


def dot(a, b):
    return jnp.dot(a, b, preferred_element_type=F32)


def dot_nt(a, b):
    return lax.dot_general(a, b, (((1,), (1,)), ((), ())), preferred_element_type=F32)


def dot_tn(a, b):
    return lax.dot_general(a, b, (((0,), (0,)), ((), ())), preferred_element_type=F32)


def split(x):
    hi = x.astype(BF16).astype(F32)
    return hi, x - hi


def iota(shape, dim):
    return lax.broadcasted_iota(jnp.int32, shape, dim)


def total(x):
    return jnp.sum(jnp.sum(x, axis=0, keepdims=True), axis=1, keepdims=True)


def stream(src, dst, sems, sizes):
    copies = {}
    at = 0
    for c, size in enumerate(sizes):
        copies[at] = pltpu.make_async_copy(src.at[pl.ds(at, size)], dst.at[pl.ds(at, size)], sems.at[c])
        at += size
    return copies


def stream_blocks(src, kept, rest, sems):
    copies = {}
    at = 0
    for c, size in enumerate(BLOCK_CHUNKS):
        if at >= KEPT:
            copies[at] = pltpu.make_async_copy(
                src.at[pl.ds(at, size)], rest.at[pl.ds(at - KEPT, size)], sems.at[c]
            )
        elif kept is not None:
            copies[at] = pltpu.make_async_copy(src.at[pl.ds(at, size)], kept.at[pl.ds(at, size)], sems.at[c])
        at += size
    return copies


class Joined:
    def __init__(self, kept, rest):
        self.kept, self.rest = kept, rest

    def __getitem__(self, e):
        return self.kept[e] if e < KEPT else self.rest[e - KEPT]


def start_order(blocks, jac):
    order = list(blocks.values())
    for one in order[:AHEAD]:
        one.start()
    then = {at: [] for at in blocks}
    for at, one in zip(blocks, order[AHEAD:]):
        then[at].append(one)
    if START_JAC < 0:
        for one in jac.values():
            one.start()
    else:
        then[START_JAC] += list(jac.values())
    return then


def block_solve(x, blocks, copies, then):
    row = iota((16, BLOCK), 0) % 8
    parts = []
    for g in range(E // 8):
        hi, lo = split(x[8 * g : 8 * g + 8])
        both = jnp.concatenate([hi, lo], axis=0)
        acc = None
        for k in range(8):
            e = 8 * g + k
            if e in copies:
                copies[e].wait()
                for later in then.get(e, ()):
                    later.start()
            one = dot(jnp.where(row == k, both, 0.0).astype(BF16), blocks[e])
            acc = one if acc is None else acc + one
        parts.append(acc[:8] + acc[8:])
    return jnp.concatenate(parts, axis=0)


def point_masks(recv_node, counts):
    elem = lax.shift_right_logical(recv_node, 6)
    node = jnp.bitwise_and(recv_node, NODES - 1)
    node_hot = (iota((NODES, RPTS), 0) == node).astype(F32).astype(BF16)
    lane = iota((1, RPTS), 1)
    block = lax.shift_right_logical(lane, 7)
    count = jnp.where(
        block == 0, counts[0], jnp.where(block == 1, counts[1], jnp.where(block == 2, counts[2], counts[3]))
    )
    live = jnp.bitwise_and(lane, 127) < count
    elem_hot = (iota((E, RPTS), 0) == jnp.where(live, elem, -1)).astype(F32)
    return node_hot, elem_hot


def pick(z, masks):
    node_hot, elem_hot = masks
    hi, lo = split(z)
    rows = [part[:, v * NODES : (v + 1) * NODES] for part in (hi, lo) for v in range(VARS)]
    rows = jnp.concatenate(rows, axis=0).astype(BF16)
    at_node = dot(rows, node_hot)
    at_node = at_node[: VARS * E] + at_node[VARS * E :]
    return [
        jnp.sum(at_node[v * E : (v + 1) * E] * elem_hot, axis=0, keepdims=True)
        for v in range(VARS)
    ]


def pack(owner_hot, rank, comps):
    slot = iota((CAP, RPTS), 0) == rank
    rows = [jnp.where(slot, comp, 0.0) for comp in comps]
    rows.append(jnp.zeros((PEERS - CAP * len(comps), RPTS), F32))
    rows = jnp.concatenate(rows, axis=0)
    hi, rest = split(rows)
    mid, low = split(rest)
    out = dot_nt(owner_hot, jnp.concatenate([hi, mid, low], axis=0).astype(BF16))
    return (out[:, :PEERS] + out[:, PEERS : 2 * PEERS]) + out[:, 2 * PEERS :]


def owner_one_hot(owners):
    return (iota((PEERS, RPTS), 0) == owners).astype(F32)


def lagrange(coord):
    factors = []
    for k in range(4):
        factor = None
        for m in range(4):
            if m != k:
                one = (coord - GLL[m]) * (1.0 / (GLL[k] - GLL[m]))
                factor = one if factor is None else factor * one
        factors.append(factor)
    return factors


def interpolate(values, geometry, table):
    values = values.T
    geometry = geometry.T
    val = [values[8 * c : 8 * c + 8] for c in range(VARS)]
    parts = [split(one) for one in val]
    coords = [geometry[8 * (VARS + c) : 8 * (VARS + c) + 8] for c in range(3)]
    rows = [one for coord in coords for one in lagrange(coord)]
    rows.append(geometry[8 * (VARS + 3) : 8 * (VARS + 3) + 8])
    rows += [part[0] for part in parts] + [part[1] for part in parts]
    for c, one in enumerate(rows):
        table[8 * c : 8 * c + 8, :] = one
    sub = iota((8, PEERS), 0)
    elem_id = iota((E, PEERS), 0).astype(F32)
    left = []
    right = []
    for k in range(CAP):

        def row(c):
            return table[pl.ds(8 * c + k, 1), :]

        inner = sub % 4
        along_z = jnp.where(
            inner == 0, row(8), jnp.where(inner == 1, row(9), jnp.where(inner == 2, row(10), row(11)))
        )
        lower = jnp.where(sub < 4, row(4), row(5)) * along_z
        upper = jnp.where(sub < 4, row(6), row(7)) * along_z
        basis = jnp.concatenate(
            [half * row(i) for i in range(4) for half in (lower, upper)], axis=0
        )
        hi, lo = split(basis)
        right.append(jnp.concatenate([hi, lo], axis=0).astype(BF16))
        mask = elem_id == row(12)
        left.append(
            jnp.concatenate(
                [jnp.where(mask, row(13 + c), 0.0) for c in range(2 * VARS)], axis=0
            ).astype(BF16)
        )
    out = dot_nt(jnp.concatenate(left, axis=1), jnp.concatenate(right, axis=1))
    half = VARS * E
    out = out[:half, :NODES] + (out[:half, NODES:] + out[half:, :NODES])
    return jnp.concatenate([out[v * E : (v + 1) * E] for v in range(VARS)], axis=1)


def face_traces(z, jac, copies, spread, traces, outs):
    hi, lo = split(z)
    traces[...] = dot_nt(jnp.concatenate([hi, lo], axis=0).astype(BF16), spread)
    own_face = iota((16, 6 * FACEW), 1) // FACEW == iota((16, 6 * FACEW), 0) % 8
    for e in range(E):
        if e in copies:
            copies[e].wait()
        both = jnp.concatenate(
            [
                jnp.broadcast_to(traces[pl.ds(e, 1), :], (8, 6 * FACEW)),
                jnp.broadcast_to(traces[pl.ds(E + e, 1), :], (8, 6 * FACEW)),
            ],
            axis=0,
        )
        one = dot(jnp.where(own_face, both, 0.0).astype(BF16), jac[e])
        outs[8 * e : 8 * e + 8, 0:FACEW] = one[:8] + one[8:]
    return jnp.concatenate(
        [outs[pl.ds(f, E, stride=8), :][:, :FACEW] for f in range(6)], axis=0
    )


def faces(x, z, jac, copies, hots, spread_ref, base_ref, first_ref, second_ref, traces, outs):
    out = face_traces(z, jac, copies, spread_ref[...], traces, outs)
    hi, lo = split(out)
    hi, lo = hi.astype(BF16), lo.astype(BF16)
    local_hot, iface_hot = hots
    outgoing = dot(iface_hot, hi) + dot(iface_hot, lo)
    odd = lax.axis_index("dom") % 2 == 1
    low, high = outgoing[:E], outgoing[E:]
    first_ref[...] = jnp.where(odd, high, low)
    second_ref[...] = jnp.where(odd, low, high)
    base_ref[...] = x - spread_faces(dot_tn(local_hot, hi), dot_tn(local_hot, lo), spread_ref)


def first_kernel(
    x_hbm, blocks_hbm, jac_hbm, node_hbm, owner_hbm, elem_hbm, coord_hbm, count_hbm, nbr_hbm, spread_hbm,
    base_ref, first_ref, second_ref, pay_hbm, rank_ref, kept_ref,
    x_ref, node_ref, owner_ref, elem_ref, coord_ref, count_ref, nbr_ref, spread_ref, small_sems,
    blocks, block_sems, jac, jac_sems, traces, outs, pay_ref, pay_sem,
):
    small = [
        pltpu.make_async_copy(src, dst, small_sems.at[i])
        for i, (src, dst) in enumerate(
            [
                (owner_hbm, owner_ref), (x_hbm, x_ref), (node_hbm, node_ref), (elem_hbm, elem_ref),
                (coord_hbm, coord_ref), (count_hbm, count_ref), (nbr_hbm, nbr_ref), (spread_hbm, spread_ref),
            ]
        )
    ]
    block_copies = stream_blocks(blocks_hbm, kept_ref, blocks, block_sems)
    jac_copies = stream(jac_hbm, jac, jac_sems, JAC_CHUNKS)
    for one in small[:2]:
        one.start()
    then = start_order(block_copies, jac_copies)
    for one in small[2:]:
        one.start()
    for one in small[:2]:
        one.wait()
    hot = owner_one_hot(owner_ref[...])
    hot16 = hot.astype(BF16)
    earlier = (iota((RPTS, RPTS), 0) < iota((RPTS, RPTS), 1)).astype(F32).astype(BF16)
    rank = jnp.sum(hot * dot(hot16, earlier), axis=0, keepdims=True).astype(jnp.int32)
    rank_ref[...] = rank
    x = x_ref[...]
    z = block_solve(x, Joined(kept_ref, blocks), block_copies, then)
    for one in small[2:]:
        one.wait()
    masks = point_masks(node_ref[...], [count_ref[0, i] for i in range(4)])
    comps = pick(z, masks)
    comps += [coord_ref[c : c + 1, :] for c in range(3)]
    comps.append(elem_ref[...].astype(F32))
    pay_ref[...] = pack(hot16, rank, comps)
    sent = pltpu.make_async_copy(pay_ref, pay_hbm, pay_sem)
    sent.start()
    faces(x, z, jac, jac_copies, neighbour_one_hots(nbr_ref[...]), spread_ref, base_ref, first_ref, second_ref, traces, outs)
    sent.wait()


def neighbour_one_hots(nbr):
    target = jnp.concatenate(
        [
            jnp.where(nbr[f : f + 1] < 0, -1, jnp.where(nbr[f : f + 1] < E, nbr[f : f + 1] + (f ^ 1) * E, nbr[f : f + 1] + 5 * E))
            for f in range(6)
        ],
        axis=1,
    )
    hot = (iota((8 * E, 6 * E), 0) == target).astype(F32).astype(BF16)
    return hot[: 6 * E], hot[6 * E :]


def spread_faces(hi, lo, spread_ref):
    acc = None
    for f in range(6):
        both = jnp.concatenate([hi[f * E : (f + 1) * E], lo[f * E : (f + 1) * E]], axis=0)
        one = dot(both.astype(BF16), spread_ref[f * FACEW : (f + 1) * FACEW, :])
        acc = one if acc is None else acc + one
    return acc[:E] + acc[E:]


def arrived(first, second, nbr, spread_ref):
    odd = lax.axis_index("dom") % 2 == 1
    low, high = jnp.where(odd, second, first), jnp.where(odd, first, second)
    hi, lo = split(jnp.concatenate([low, high], axis=0))
    _, iface_hot = neighbour_one_hots(nbr)
    hi, lo = dot_tn(iface_hot, hi.astype(BF16)), dot_tn(iface_hot, lo.astype(BF16))
    return spread_faces(hi, lo, spread_ref)


def late_interp_kernel(got_ref, first_ref, out_ref, table):
    out_ref[...] = interpolate(got_ref[...], first_ref[...], table)


def interp_kernel(got_ref, blocks_hbm, interp_ref, blocks_ref, table, sems):
    copies = list(stream_blocks(blocks_hbm, None, blocks_ref, sems).values())
    for one in copies:
        one.start()
    got = got_ref[...]
    interp_ref[...] = interpolate(got, got, table)
    for one in copies:
        one.wait()


def with_scalars(table, scalars):
    lane = iota(table.shape, 1)
    for i, one in enumerate(scalars):
        table = jnp.where(lane == SCALAR_LANE + i, one, table)
    return table


def read_scalars(table, count):
    row = jnp.sum(table, axis=0, keepdims=True)
    return [row[:, SCALAR_LANE + i : SCALAR_LANE + i + 1] for i in range(count)]


def second_kernel(
    base_ref, first_in, second_in, interp_ref, b_ref, kept_ref, blocks_ref, jac_hbm,
    node_ref, owner_ref, rank_ref, count_ref, nbr_ref, spread_ref,
    u_ref, out_ref, first_ref, second_ref, pay_hbm,
    jac, jac_sems, traces, outs, pay_ref, pay_sem,
):
    jac_copies = stream(jac_hbm, jac, jac_sems, (16, 16))
    for one in jac_copies.values():
        one.start()
    b = b_ref[...]
    nbr = nbr_ref[...]
    u = base_ref[...] - interp_ref[...] - arrived(first_in[...], second_in[...], nbr, spread_ref)
    u_ref[...] = u
    scalars = [total(b * b), total(b * u)]
    z = block_solve(u, Joined(kept_ref, blocks_ref), {}, {})
    jac_copies.pop(0).wait()
    masks = point_masks(node_ref[...], [count_ref[0, i] for i in range(4)])
    hot = owner_one_hot(owner_ref[...]).astype(BF16)
    pay_ref[...] = with_scalars(pack(hot, rank_ref[...], pick(z, masks)), scalars)
    sent = pltpu.make_async_copy(pay_ref, pay_hbm, pay_sem)
    sent.start()
    jac_copies.pop(16).wait()
    faces(u, z, jac, jac_copies, neighbour_one_hots(nbr), spread_ref, out_ref, first_ref, second_ref, traces, outs)
    sent.wait()


def third_kernel(
    base_ref, first_ref, second_ref, nbr_ref, spread_ref, interp_ref, got_ref, b_ref, u_ref,
    rest_ref, pay_ref, known_ref,
):
    late = arrived(first_ref[...], second_ref[...], nbr_ref[...], spread_ref)
    w = base_ref[...] - interp_ref[...] - late
    bb, bu = read_scalars(got_ref[...], 2)
    h00 = bu / (bb + EPS)
    b = b_ref[...]
    u = u_ref[...]
    rest = u - h00 * b
    mapped = w - h00 * u
    rest_ref[...] = rest
    scalars = [
        total(rest * rest), total(b * rest), total(mapped * b), total(mapped * rest), total(mapped * mapped),
    ]
    pay_ref[...] = with_scalars(jnp.zeros((PEERS, PEERS), F32), scalars)
    known_ref[...] = with_scalars(jnp.zeros((8, PEERS), F32), [bb * 0.125, bu * 0.125])


def last_kernel(got_ref, known_ref, b_ref, rest_ref, out_ref):
    bb, bu = read_scalars(known_ref[...], 2)
    rr, br, mb, mr, mm = read_scalars(got_ref[...], 5)
    s2 = bb + EPS
    start = jnp.sqrt(s2)
    h00 = bu / s2
    h10 = jnp.sqrt(rr / s2 + EPS)
    h01 = mb / (s2 * h10)
    scale = s2 * (h10 * h10)
    h11 = mr / scale
    left = (
        mm / scale
        - h01 * h01 * (2.0 - bb / s2)
        - h11 * h11 * (2.0 - rr / scale)
        + 2.0 * h01 * h11 * (br / (s2 * h10))
    )
    h21 = jnp.sqrt(jnp.maximum(left, 0.0) + EPS)
    r00 = jnp.sqrt(h00 * h00 + h10 * h10)
    c0 = h00 / r00
    s0 = h10 / r00
    r01 = c0 * h01 + s0 * h11
    low = c0 * h11 - s0 * h01
    r11 = jnp.sqrt(low * low + h21 * h21)
    c1 = low / r11
    y1 = c1 * (-s0 * start) / r11
    y0 = (c0 * start - r01 * y1) / r00
    out_ref[...] = (y0 / start) * b_ref[...] + (y1 / (start * h10)) * rest_ref[...]


VM = pl.BlockSpec(memory_space=pltpu.VMEM)
SM = pl.BlockSpec(memory_space=pltpu.SMEM)


HBM = pl.BlockSpec(memory_space=pltpu.HBM)


def swaps(start, ends):
    return [pair for i in range(start, ends, 2) for pair in ((i, i + 1), (i + 1, i))]


def in_hbm(x):
    return pltpu.with_memory_space_constraint(x, pltpu.HBM)


def call(kernel, in_specs, outs, scratch, *args, hbm_out=None):
    return pl.pallas_call(
        kernel,
        in_specs=in_specs,
        out_specs=[HBM if i == hbm_out else VM for i in range(len(outs))],
        out_shape=[jax.ShapeDtypeStruct(shape, dtype) for shape, dtype in outs],
        scratch_shapes=scratch,
        compiler_params=pltpu.CompilerParams(vmem_limit_bytes=VMEM_LIMIT),
        name=kernel.__name__,
    )(*args)


def exchange(table):
    return lax.all_to_all(
        table.reshape(PEERS, 1, PEERS), AXES, split_axis=0, concat_axis=0, tiled=True
    ).reshape(PEERS, PEERS)


def local(
    grad_rhs, block_inv, face_jac, face_nbr, recv_node, owners, donor_elem, donor_coords, recv_counts
):
    jac = face_jac.reshape(E, 6 * FACEW, FACEW)
    nbr = face_nbr.T
    node = recv_node.reshape(1, RPTS)
    owner = owners.reshape(1, RPTS)
    elem = donor_elem.reshape(1, RPTS)
    spread = jnp.asarray(spread_matrix(), BF16)
    ends = lax.axis_size("dom") - 1
    even_pairs = swaps(0, ends)
    odd_pairs = swaps(1, ends)
    full = ((E, BLOCK), F32)
    table = ((PEERS, PEERS), F32)
    half = ((E, FACEW), F32)
    row = pltpu.VMEM((1, RPTS), jnp.int32)
    matrices = [
        pltpu.VMEM((E - KEPT, BLOCK, BLOCK), BF16), pltpu.SemaphoreType.DMA((len(BLOCK_CHUNKS),)),
        pltpu.VMEM((E, 6 * FACEW, FACEW), BF16), pltpu.SemaphoreType.DMA((2,)),
    ]
    pay_scratch = [pltpu.VMEM((PEERS, PEERS), F32), pltpu.SemaphoreType.DMA]
    face_scratch = [pltpu.VMEM((2 * E, 6 * FACEW), F32), pltpu.VMEM((8 * E, PEERS), F32)]
    rows_scratch = pltpu.VMEM((8 * (13 + 2 * VARS), PEERS), F32)

    def swap(first, second):
        return lax.ppermute(first, "dom", odd_pairs), lax.ppermute(second, "dom", even_pairs)

    small = (node, owner, elem, donor_coords, recv_counts, nbr, spread)
    base, first, second, pay, rank, kept = call(
        first_kernel,
        [HBM] * 10,
        [full, half, half, table, ((1, RPTS), jnp.int32), ((KEPT, BLOCK, BLOCK), BF16)],
        [
            pltpu.VMEM((E, BLOCK), F32), row, row, row, pltpu.VMEM((3, RPTS), F32),
            pltpu.SMEM((1, 4), jnp.int32), pltpu.VMEM((6, E), jnp.int32),
            pltpu.VMEM((6 * FACEW, BLOCK), BF16), pltpu.SemaphoreType.DMA((8,)),
        ]
        + matrices
        + face_scratch
        + pay_scratch,
        *[in_hbm(one) for one in (grad_rhs, block_inv, jac) + small],
        hbm_out=3,
    )
    got1 = exchange(pay)
    first, second = swap(first, second)
    interp, blocks = call(
        interp_kernel,
        [VM, HBM],
        [full, ((E - KEPT, BLOCK, BLOCK), BF16)],
        [rows_scratch, matrices[1]],
        got1, in_hbm(block_inv),
    )
    u, base, first, second, pay = call(
        second_kernel,
        [VM] * 7 + [HBM] + [VM] * 3 + [SM, VM, VM],
        [full, full, half, half, table],
        matrices[2:] + face_scratch + pay_scratch,
        base, first, second, interp, grad_rhs, kept, blocks, in_hbm(jac), node, owner, rank, recv_counts, nbr, spread,
        hbm_out=4,
    )
    got2 = exchange(pay)
    first, second = swap(first, second)
    interp = call(late_interp_kernel, [VM, VM], [full], [rows_scratch], got2, got1)[0]
    rest, pay, known = call(
        third_kernel,
        [VM] * 9,
        [full, table, ((8, PEERS), F32)],
        [],
        base, first, second, nbr, spread, interp, got2, grad_rhs, u,
    )
    got3 = exchange(pay)
    return call(last_kernel, [VM] * 4, [full], [], got3, known, grad_rhs, rest)[0]


def solution(mesh):
    placed = (
        P(AXES, None),
        P(AXES, None, None),
        P(AXES, None, None, None),
        P(AXES, None),
        P(AXES),
        P(AXES, None),
        P(AXES),
        P(None, AXES),
        P(AXES, None),
    )
    return jax.shard_map(
        local, mesh=mesh, in_specs=placed, out_specs=P(AXES, None), check_vma=False
    )
```

```python
import jax
import jax.numpy as jnp
import numpy as np
from jax import lax
from jax.experimental import pallas as pl
from jax.experimental.pallas import tpu as pltpu
from jax.sharding import PartitionSpec as P

AXES = ("grp", "dom")
VARS = 5
NODES = 64
BLOCK = 320
FACEW = 80
E = 32
PEERS = 128
CAP = 8
RPTS = 512
BLOCK_CHUNKS = (8, 16, 8)
KEPT = 8
START_JAC = 8
AHEAD = 3
JAC_CHUNKS = (16, 16)
SCALAR_LANE = 96
GLL = (-1.0, -0.4472135954999579, 0.4472135954999579, 1.0)
EPS = 1e-06
F32 = jnp.float32
BF16 = jnp.bfloat16
VMEM_LIMIT = 24 * 1024 * 1024


def face_table():
    grid = np.arange(64).reshape(4, 4, 4)
    faces = [grid[0], grid[3], grid[:, 0], grid[:, 3], grid[:, :, 0], grid[:, :, 3]]
    return np.stack([one.reshape(16) for one in faces])


def spread_matrix():
    table = face_table()
    out = np.zeros((6, VARS, 16, BLOCK), np.float32)
    for f in range(6):
        for v in range(VARS):
            out[f, v, np.arange(16), v * NODES + table[f]] = 1.0
    return out.reshape(6 * FACEW, BLOCK)


def dot(a, b):
    return jnp.dot(a, b, preferred_element_type=F32)


def dot_nt(a, b):
    return lax.dot_general(a, b, (((1,), (1,)), ((), ())), preferred_element_type=F32)


def dot_tn(a, b):
    return lax.dot_general(a, b, (((0,), (0,)), ((), ())), preferred_element_type=F32)


def split(x):
    hi = x.astype(BF16).astype(F32)
    return hi, x - hi


def iota(shape, dim):
    return lax.broadcasted_iota(jnp.int32, shape, dim)


def total(x):
    return jnp.sum(jnp.sum(x, axis=0, keepdims=True), axis=1, keepdims=True)


def stream(src, dst, sems, sizes):
    copies = {}
    at = 0
    for c, size in enumerate(sizes):
        copies[at] = pltpu.make_async_copy(src.at[pl.ds(at, size)], dst.at[pl.ds(at, size)], sems.at[c])
        at += size
    return copies


def stream_blocks(src, kept, rest, sems):
    copies = {}
    at = 0
    for c, size in enumerate(BLOCK_CHUNKS):
        if at >= KEPT:
            copies[at] = pltpu.make_async_copy(
                src.at[pl.ds(at, size)], rest.at[pl.ds(at - KEPT, size)], sems.at[c]
            )
        elif kept is not None:
            copies[at] = pltpu.make_async_copy(src.at[pl.ds(at, size)], kept.at[pl.ds(at, size)], sems.at[c])
        at += size
    return copies


class Joined:
    def __init__(self, kept, rest):
        self.kept, self.rest = kept, rest

    def __getitem__(self, e):
        return self.kept[e] if e < KEPT else self.rest[e - KEPT]


def start_order(blocks, jac):
    order = list(blocks.values())
    for one in order[:AHEAD]:
        one.start()
    then = {at: [] for at in blocks}
    for at, one in zip(blocks, order[AHEAD:]):
        then[at].append(one)
    if START_JAC < 0:
        for one in jac.values():
            one.start()
    else:
        then[START_JAC] += list(jac.values())
    return then


def block_solve(x, blocks, copies, then):
    row = iota((16, BLOCK), 0) % 8
    parts = []
    for g in range(E // 8):
        hi, lo = split(x[8 * g : 8 * g + 8])
        both = jnp.concatenate([hi, lo], axis=0)
        acc = None
        for k in range(8):
            e = 8 * g + k
            if e in copies:
                copies[e].wait()
                for later in then.get(e, ()):
                    later.start()
            one = dot(jnp.where(row == k, both, 0.0).astype(BF16), blocks[e])
            acc = one if acc is None else acc + one
        parts.append(acc[:8] + acc[8:])
    return jnp.concatenate(parts, axis=0)


def point_masks(recv_node, counts):
    elem = lax.shift_right_logical(recv_node, 6)
    node = jnp.bitwise_and(recv_node, NODES - 1)
    node_hot = (iota((NODES, RPTS), 0) == node).astype(F32).astype(BF16)
    lane = iota((1, RPTS), 1)
    block = lax.shift_right_logical(lane, 7)
    count = jnp.where(
        block == 0, counts[0], jnp.where(block == 1, counts[1], jnp.where(block == 2, counts[2], counts[3]))
    )
    live = jnp.bitwise_and(lane, 127) < count
    elem_hot = (iota((E, RPTS), 0) == jnp.where(live, elem, -1)).astype(F32)
    return node_hot, elem_hot


def pick(z, masks):
    node_hot, elem_hot = masks
    hi, lo = split(z)
    rows = [part[:, v * NODES : (v + 1) * NODES] for part in (hi, lo) for v in range(VARS)]
    rows = jnp.concatenate(rows, axis=0).astype(BF16)
    at_node = dot(rows, node_hot)
    at_node = at_node[: VARS * E] + at_node[VARS * E :]
    return [
        jnp.sum(at_node[v * E : (v + 1) * E] * elem_hot, axis=0, keepdims=True)
        for v in range(VARS)
    ]


def pack(owner_hot, rank, comps):
    slot = iota((CAP, RPTS), 0) == rank
    rows = [jnp.where(slot, comp, 0.0) for comp in comps]
    rows.append(jnp.zeros((PEERS - CAP * len(comps), RPTS), F32))
    rows = jnp.concatenate(rows, axis=0)
    hi, rest = split(rows)
    mid, low = split(rest)
    out = dot_nt(owner_hot, jnp.concatenate([hi, mid, low], axis=0).astype(BF16))
    return (out[:, :PEERS] + out[:, PEERS : 2 * PEERS]) + out[:, 2 * PEERS :]


def owner_one_hot(owners):
    return (iota((PEERS, RPTS), 0) == owners).astype(F32)


def lagrange(coord):
    factors = []
    for k in range(4):
        factor = None
        for m in range(4):
            if m != k:
                one = (coord - GLL[m]) * (1.0 / (GLL[k] - GLL[m]))
                factor = one if factor is None else factor * one
        factors.append(factor)
    return factors


def interpolate(values, geometry, table):
    values = values.T
    geometry = geometry.T
    val = [values[8 * c : 8 * c + 8] for c in range(VARS)]
    parts = [split(one) for one in val]
    coords = [geometry[8 * (VARS + c) : 8 * (VARS + c) + 8] for c in range(3)]
    rows = [one for coord in coords for one in lagrange(coord)]
    rows.append(geometry[8 * (VARS + 3) : 8 * (VARS + 3) + 8])
    rows += [part[0] for part in parts] + [part[1] for part in parts]
    for c, one in enumerate(rows):
        table[8 * c : 8 * c + 8, :] = one
    sub = iota((8, PEERS), 0)
    elem_id = iota((E, PEERS), 0).astype(F32)
    left = []
    right = []
    for k in range(CAP):

        def row(c):
            return table[pl.ds(8 * c + k, 1), :]

        inner = sub % 4
        along_z = jnp.where(
            inner == 0, row(8), jnp.where(inner == 1, row(9), jnp.where(inner == 2, row(10), row(11)))
        )
        lower = jnp.where(sub < 4, row(4), row(5)) * along_z
        upper = jnp.where(sub < 4, row(6), row(7)) * along_z
        basis = jnp.concatenate(
            [half * row(i) for i in range(4) for half in (lower, upper)], axis=0
        )
        hi, lo = split(basis)
        right.append(jnp.concatenate([hi, lo], axis=0).astype(BF16))
        mask = elem_id == row(12)
        left.append(
            jnp.concatenate(
                [jnp.where(mask, row(13 + c), 0.0) for c in range(2 * VARS)], axis=0
            ).astype(BF16)
        )
    out = dot_nt(jnp.concatenate(left, axis=1), jnp.concatenate(right, axis=1))
    half = VARS * E
    out = out[:half, :NODES] + (out[:half, NODES:] + out[half:, :NODES])
    return jnp.concatenate([out[v * E : (v + 1) * E] for v in range(VARS)], axis=1)


def face_traces(z, jac, copies, spread, traces, outs):
    hi, lo = split(z)
    traces[...] = dot_nt(jnp.concatenate([hi, lo], axis=0).astype(BF16), spread)
    own_face = iota((16, 6 * FACEW), 1) // FACEW == iota((16, 6 * FACEW), 0) % 8
    for e in range(E):
        if e in copies:
            copies[e].wait()
        both = jnp.concatenate(
            [
                jnp.broadcast_to(traces[pl.ds(e, 1), :], (8, 6 * FACEW)),
                jnp.broadcast_to(traces[pl.ds(E + e, 1), :], (8, 6 * FACEW)),
            ],
            axis=0,
        )
        one = dot(jnp.where(own_face, both, 0.0).astype(BF16), jac[e])
        outs[8 * e : 8 * e + 8, 0:FACEW] = one[:8] + one[8:]
    return jnp.concatenate(
        [outs[pl.ds(f, E, stride=8), :][:, :FACEW] for f in range(6)], axis=0
    )


def faces(x, z, jac, copies, hots, spread_ref, base_ref, first_ref, second_ref, traces, outs):
    out = face_traces(z, jac, copies, spread_ref[...], traces, outs)
    hi, lo = split(out)
    hi, lo = hi.astype(BF16), lo.astype(BF16)
    local_hot, iface_hot = hots
    outgoing = dot(iface_hot, hi) + dot(iface_hot, lo)
    odd = lax.axis_index("dom") % 2 == 1
    low, high = outgoing[:E], outgoing[E:]
    first_ref[...] = jnp.where(odd, high, low)
    second_ref[...] = jnp.where(odd, low, high)
    base_ref[...] = x - spread_faces(dot_tn(local_hot, hi), dot_tn(local_hot, lo), spread_ref)


def first_kernel(
    x_hbm, blocks_hbm, jac_hbm, node_hbm, owner_hbm, elem_hbm, coord_hbm, count_hbm, nbr_hbm, spread_hbm,
    base_ref, first_ref, second_ref, pay_hbm, rank_ref, kept_ref,
    x_ref, node_ref, owner_ref, elem_ref, coord_ref, count_ref, nbr_ref, spread_ref, small_sems,
    blocks, block_sems, jac, jac_sems, traces, outs, pay_ref, pay_sem,
):
    small = [
        pltpu.make_async_copy(src, dst, small_sems.at[i])
        for i, (src, dst) in enumerate(
            [
                (owner_hbm, owner_ref), (x_hbm, x_ref), (node_hbm, node_ref), (elem_hbm, elem_ref),
                (coord_hbm, coord_ref), (count_hbm, count_ref), (nbr_hbm, nbr_ref), (spread_hbm, spread_ref),
            ]
        )
    ]
    block_copies = stream_blocks(blocks_hbm, kept_ref, blocks, block_sems)
    jac_copies = stream(jac_hbm, jac, jac_sems, JAC_CHUNKS)
    for one in small[:2]:
        one.start()
    then = start_order(block_copies, jac_copies)
    for one in small[2:]:
        one.start()
    for one in small[:2]:
        one.wait()
    hot = owner_one_hot(owner_ref[...])
    hot16 = hot.astype(BF16)
    earlier = (iota((RPTS, RPTS), 0) < iota((RPTS, RPTS), 1)).astype(F32).astype(BF16)
    rank = jnp.sum(hot * dot(hot16, earlier), axis=0, keepdims=True).astype(jnp.int32)
    rank_ref[...] = rank
    x = x_ref[...]
    z = block_solve(x, Joined(kept_ref, blocks), block_copies, then)
    for one in small[2:]:
        one.wait()
    masks = point_masks(node_ref[...], [count_ref[0, i] for i in range(4)])
    comps = pick(z, masks)
    comps += [coord_ref[c : c + 1, :] for c in range(3)]
    comps.append(elem_ref[...].astype(F32))
    pay_ref[...] = pack(hot16, rank, comps)
    sent = pltpu.make_async_copy(pay_ref, pay_hbm, pay_sem)
    sent.start()
    faces(x, z, jac, jac_copies, neighbour_one_hots(nbr_ref[...]), spread_ref, base_ref, first_ref, second_ref, traces, outs)
    sent.wait()


def neighbour_one_hots(nbr):
    target = jnp.concatenate(
        [
            jnp.where(nbr[f : f + 1] < 0, -1, jnp.where(nbr[f : f + 1] < E, nbr[f : f + 1] + (f ^ 1) * E, nbr[f : f + 1] + 5 * E))
            for f in range(6)
        ],
        axis=1,
    )
    hot = (iota((8 * E, 6 * E), 0) == target).astype(F32).astype(BF16)
    return hot[: 6 * E], hot[6 * E :]


def spread_faces(hi, lo, spread_ref):
    acc = None
    for f in range(6):
        both = jnp.concatenate([hi[f * E : (f + 1) * E], lo[f * E : (f + 1) * E]], axis=0)
        one = dot(both.astype(BF16), spread_ref[f * FACEW : (f + 1) * FACEW, :])
        acc = one if acc is None else acc + one
    return acc[:E] + acc[E:]


def arrived(first, second, nbr, spread_ref):
    odd = lax.axis_index("dom") % 2 == 1
    low, high = jnp.where(odd, second, first), jnp.where(odd, first, second)
    hi, lo = split(jnp.concatenate([low, high], axis=0))
    _, iface_hot = neighbour_one_hots(nbr)
    hi, lo = dot_tn(iface_hot, hi.astype(BF16)), dot_tn(iface_hot, lo.astype(BF16))
    return spread_faces(hi, lo, spread_ref)


def late_interp_kernel(got_ref, first_ref, out_ref, table):
    out_ref[...] = interpolate(got_ref[...], first_ref[...], table)


def interp_kernel(got_ref, blocks_hbm, interp_ref, blocks_ref, table, sems):
    copies = list(stream_blocks(blocks_hbm, None, blocks_ref, sems).values())
    for one in copies:
        one.start()
    got = got_ref[...]
    interp_ref[...] = interpolate(got, got, table)
    for one in copies:
        one.wait()


def with_scalars(table, scalars):
    lane = iota(table.shape, 1)
    for i, one in enumerate(scalars):
        table = jnp.where(lane == SCALAR_LANE + i, one, table)
    return table


def read_scalars(table, count):
    row = jnp.sum(table, axis=0, keepdims=True)
    return [row[:, SCALAR_LANE + i : SCALAR_LANE + i + 1] for i in range(count)]


def second_kernel(
    base_ref, first_in, second_in, interp_ref, b_ref, kept_ref, blocks_ref, jac_hbm,
    node_ref, owner_ref, rank_ref, count_ref, nbr_ref, spread_ref,
    u_ref, out_ref, first_ref, second_ref, pay_hbm,
    jac, jac_sems, traces, outs, pay_ref, pay_sem,
):
    jac_copies = stream(jac_hbm, jac, jac_sems, (16, 16))
    for one in jac_copies.values():
        one.start()
    b = b_ref[...]
    nbr = nbr_ref[...]
    u = base_ref[...] - interp_ref[...] - arrived(first_in[...], second_in[...], nbr, spread_ref)
    u_ref[...] = u
    scalars = [total(b * b), total(b * u)]
    z = block_solve(u, Joined(kept_ref, blocks_ref), {}, {})
    jac_copies.pop(0).wait()
    masks = point_masks(node_ref[...], [count_ref[0, i] for i in range(4)])
    hot = owner_one_hot(owner_ref[...]).astype(BF16)
    pay_ref[...] = with_scalars(pack(hot, rank_ref[...], pick(z, masks)), scalars)
    sent = pltpu.make_async_copy(pay_ref, pay_hbm, pay_sem)
    sent.start()
    jac_copies.pop(16).wait()
    faces(u, z, jac, jac_copies, neighbour_one_hots(nbr), spread_ref, out_ref, first_ref, second_ref, traces, outs)
    sent.wait()


def third_kernel(
    base_ref, first_ref, second_ref, nbr_ref, spread_ref, interp_ref, got_ref, b_ref, u_ref,
    rest_ref, pay_ref, known_ref,
):
    late = arrived(first_ref[...], second_ref[...], nbr_ref[...], spread_ref)
    w = base_ref[...] - interp_ref[...] - late
    bb, bu = read_scalars(got_ref[...], 2)
    h00 = bu / (bb + EPS)
    b = b_ref[...]
    u = u_ref[...]
    rest = u - h00 * b
    mapped = w - h00 * u
    rest_ref[...] = rest
    scalars = [
        total(rest * rest), total(b * rest), total(mapped * b), total(mapped * rest), total(mapped * mapped),
    ]
    pay_ref[...] = with_scalars(jnp.zeros((PEERS, PEERS), F32), scalars)
    known_ref[...] = with_scalars(jnp.zeros((8, PEERS), F32), [bb * 0.125, bu * 0.125])


def last_kernel(got_ref, known_ref, b_ref, rest_ref, out_ref):
    bb, bu = read_scalars(known_ref[...], 2)
    rr, br, mb, mr, mm = read_scalars(got_ref[...], 5)
    s2 = bb + EPS
    start = jnp.sqrt(s2)
    h00 = bu / s2
    h10 = jnp.sqrt(rr / s2 + EPS)
    h01 = mb / (s2 * h10)
    scale = s2 * (h10 * h10)
    h11 = mr / scale
    left = (
        mm / scale
        - h01 * h01 * (2.0 - bb / s2)
        - h11 * h11 * (2.0 - rr / scale)
        + 2.0 * h01 * h11 * (br / (s2 * h10))
    )
    h21 = jnp.sqrt(jnp.maximum(left, 0.0) + EPS)
    r00 = jnp.sqrt(h00 * h00 + h10 * h10)
    c0 = h00 / r00
    s0 = h10 / r00
    r01 = c0 * h01 + s0 * h11
    low = c0 * h11 - s0 * h01
    r11 = jnp.sqrt(low * low + h21 * h21)
    c1 = low / r11
    y1 = c1 * (-s0 * start) / r11
    y0 = (c0 * start - r01 * y1) / r00
    out_ref[...] = (y0 / start) * b_ref[...] + (y1 / (start * h10)) * rest_ref[...]


VM = pl.BlockSpec(memory_space=pltpu.VMEM)
SM = pl.BlockSpec(memory_space=pltpu.SMEM)


HBM = pl.BlockSpec(memory_space=pltpu.HBM)


def swaps(start, ends):
    return [pair for i in range(start, ends, 2) for pair in ((i, i + 1), (i + 1, i))]


def in_hbm(x):
    return pltpu.with_memory_space_constraint(x, pltpu.HBM)


def call(kernel, in_specs, outs, scratch, *args, hbm_out=None):
    return pl.pallas_call(
        kernel,
        in_specs=in_specs,
        out_specs=[HBM if i == hbm_out else VM for i in range(len(outs))],
        out_shape=[jax.ShapeDtypeStruct(shape, dtype) for shape, dtype in outs],
        scratch_shapes=scratch,
        compiler_params=pltpu.CompilerParams(vmem_limit_bytes=VMEM_LIMIT),
        name=kernel.__name__,
    )(*args)


def exchange(table):
    return lax.all_to_all(
        table.reshape(PEERS, 1, PEERS), AXES, split_axis=0, concat_axis=0, tiled=True
    ).reshape(PEERS, PEERS)


def local(
    grad_rhs, block_inv, face_jac, face_nbr, recv_node, owners, donor_elem, donor_coords, recv_counts
):
    jac = face_jac.reshape(E, 6 * FACEW, FACEW)
    nbr = face_nbr.T
    node = recv_node.reshape(1, RPTS)
    owner = owners.reshape(1, RPTS)
    elem = donor_elem.reshape(1, RPTS)
    spread = jnp.asarray(spread_matrix(), BF16)
    ends = lax.axis_size("dom") - 1
    even_pairs = swaps(0, ends)
    odd_pairs = swaps(1, ends)
    full = ((E, BLOCK), F32)
    table = ((PEERS, PEERS), F32)
    half = ((E, FACEW), F32)
    row = pltpu.VMEM((1, RPTS), jnp.int32)
    matrices = [
        pltpu.VMEM((E - KEPT, BLOCK, BLOCK), BF16), pltpu.SemaphoreType.DMA((len(BLOCK_CHUNKS),)),
        pltpu.VMEM((E, 6 * FACEW, FACEW), BF16), pltpu.SemaphoreType.DMA((2,)),
    ]
    pay_scratch = [pltpu.VMEM((PEERS, PEERS), F32), pltpu.SemaphoreType.DMA]
    face_scratch = [pltpu.VMEM((2 * E, 6 * FACEW), F32), pltpu.VMEM((8 * E, PEERS), F32)]
    rows_scratch = pltpu.VMEM((8 * (13 + 2 * VARS), PEERS), F32)

    def swap(first, second):
        return lax.ppermute(first, "dom", odd_pairs), lax.ppermute(second, "dom", even_pairs)

    small = (node, owner, elem, donor_coords, recv_counts, nbr, spread)
    base, first, second, pay, rank, kept = call(
        first_kernel,
        [HBM] * 10,
        [full, half, half, table, ((1, RPTS), jnp.int32), ((KEPT, BLOCK, BLOCK), BF16)],
        [
            pltpu.VMEM((E, BLOCK), F32), row, row, row, pltpu.VMEM((3, RPTS), F32),
            pltpu.SMEM((1, 4), jnp.int32), pltpu.VMEM((6, E), jnp.int32),
            pltpu.VMEM((6 * FACEW, BLOCK), BF16), pltpu.SemaphoreType.DMA((8,)),
        ]
        + matrices
        + face_scratch
        + pay_scratch,
        *[in_hbm(one) for one in (grad_rhs, block_inv, jac) + small],
        hbm_out=3,
    )
    got1 = exchange(pay)
    first, second = swap(first, second)
    interp, blocks = call(
        interp_kernel,
        [VM, HBM],
        [full, ((E - KEPT, BLOCK, BLOCK), BF16)],
        [rows_scratch, matrices[1]],
        got1, in_hbm(block_inv),
    )
    u, base, first, second, pay = call(
        second_kernel,
        [VM] * 7 + [HBM] + [VM] * 3 + [SM, VM, VM],
        [full, full, half, half, table],
        matrices[2:] + face_scratch + pay_scratch,
        base, first, second, interp, grad_rhs, kept, blocks, in_hbm(jac), node, owner, rank, recv_counts, nbr, spread,
        hbm_out=4,
    )
    got2 = exchange(pay)
    first, second = swap(first, second)
    interp = call(late_interp_kernel, [VM, VM], [full], [rows_scratch], got2, got1)[0]
    rest, pay, known = call(
        third_kernel,
        [VM] * 9,
        [full, table, ((8, PEERS), F32)],
        [],
        base, first, second, nbr, spread, interp, got2, grad_rhs, u,
    )
    got3 = exchange(pay)
    return call(last_kernel, [VM] * 4, [full], [], got3, known, grad_rhs, rest)[0]


def solution(mesh):
    placed = (
        P(AXES, None),
        P(AXES, None, None),
        P(AXES, None, None, None),
        P(AXES, None),
        P(AXES),
        P(AXES, None),
        P(AXES),
        P(None, AXES),
        P(AXES, None),
    )
    return jax.shard_map(
        local, mesh=mesh, in_specs=placed, out_specs=P(AXES, None), check_vma=False
    )
```
